256 devices in a mesh: band: 32 (over z, x), dom: 8 (over y, core).
Axes of the slice: x: 4, y: 4, z: 8, core: 2. Of those that a mesh axis runs over, the one named last changes fastest.
Arguments:
- orbitals: bfloat16 [512, 32, 2048], P('band', 'dom'), may hold values from -6 to 6
- potential: float32 [32, 2048], P('dom'), may hold values from 0 to 2
- bounds: float32 [2], replicated, may hold values from 1 to 10, as said below
Outputs:
- rotated: bfloat16 [512, 32, 2048], P('band', 'dom')
- projected: float32 [512, 512], replicated
The draws below stay inside these ranges and needn't reach their ends.
Inputs may be any that keep to these rules, and one draw needn't show every extreme that they name: bounds[0] lies in 1 to 2 and bounds[1] in 8.5 to 10, above the whole spectrum of H.
All inputs are finite; a program needn't handle non-finite values.
Results may differ from the reference program's by a relative error of at most 0.006.
Values may be sent and summed in bfloat16 or wider, within the bound.
No kernel may reach another device: no remote copies, remote signals or barrier semaphores. Data moves between devices by JAX's collectives and lax.ppermute only.
A program may use at most 64 MiB of HBM per device.

```python
import math
import jax
import jax.numpy as jnp
from jax import lax

BANDS = 512
GRID_Y = 64
GRID_Z = 32
DEG = 8
NS_STEPS = 8
GRID_X = 32
GRID_YZ = 2048


def draw_bounds(key, part):
    first_key, second_key = jax.random.split(jax.random.fold_in(key, 17))
    lower_cut = jax.random.uniform(first_key, (), jnp.float32, 1.0, 2.0)
    upper_cut = jax.random.uniform(second_key, (), jnp.float32, 8.5, 10.0)
    return jnp.stack([lower_cut, upper_cut]).astype(jnp.float32)


def block_scale(rng, extent, pieces, smallest, largest):
    factor_of = 1.0
    for dim, parts in pieces:
        steps = jax.random.uniform(jax.random.fold_in(jax.random.fold_in(rng, 6), dim), (parts,), jnp.float32, smallest / len(pieces), largest / len(pieces))
        factor_of = factor_of * jnp.repeat(jnp.exp(steps), extent[dim] // parts).reshape((-1,) + (1,) * (len(extent) - 1 - dim))
    return factor_of


def centred(key, dims, width, bound, pieces=(), kind=jnp.bfloat16):
    entries = jax.random.normal(key, dims, jnp.float32) * width
    if len(pieces) > 0:
        entries = block_scale(key, dims, pieces, -0.22, 0.18) * entries
    return jnp.clip(entries, min=-bound, max=bound).astype(kind)


def setup_inputs(seed: int = 0) -> dict:
    key_of = jax.random.split(jax.random.key(seed), 4)
    orbitals = centred(key_of[0], (BANDS, GRID_X, GRID_YZ), 1.0, 6.0, ((0, 32), (1, 8)))
    potential = jnp.clip(2.0 * jax.random.uniform(key_of[1], (GRID_X, GRID_YZ), jnp.float32) ** block_scale(key_of[1], (GRID_X, GRID_YZ), ((0, 8),), -0.2, 0.2), 0.0, 2.0)
    bounds = draw_bounds(jax.random.fold_in(key_of[3], 71), 0)
    return dict(orbitals=orbitals, potential=potential, bounds=bounds)


def hamiltonian(field, pot_grid):
    beside = jnp.roll(field, -1, 1) + jnp.roll(field, 1, 1)
    beside = beside + jnp.roll(field, -1, 2) + jnp.roll(field, 1, 2)
    beside = beside + jnp.roll(field, -1, 3) + jnp.roll(field, 1, 3)
    return -0.5 * (beside - 6.0 * field) + pot_grid * field

def filter_group(orbital_block, pot_grid, lower_cut, upper_cut):
    half_width = (upper_cut - lower_cut) / 2.0
    centre = (upper_cut + lower_cut) / 2.0
    start = orbital_block.astype(jnp.float32)
    earlier = start
    current = (hamiltonian(start, pot_grid) - centre * start) / half_width
    for repeat in range(DEG - 1):
        following = 2.0 * (hamiltonian(current, pot_grid) - centre * current) / half_width - earlier
        earlier = current
        current = following
    applied = hamiltonian(current, pot_grid)
    return (current.astype(jnp.bfloat16), applied.astype(jnp.bfloat16))

def reference(orbitals, potential, bounds):
    grid_x = orbitals.shape[1]
    group_size = math.gcd(BANDS, 64)
    pot_grid = potential.reshape(grid_x, GRID_Y, GRID_Z)
    blocks = orbitals.reshape(BANDS // group_size, group_size, grid_x, GRID_Y, GRID_Z)
    lower_cut = bounds[0]
    upper_cut = bounds[1]
    filt, applied = lax.map(lambda item: filter_group(item, pot_grid, lower_cut, upper_cut), blocks)
    points = grid_x * GRID_Y * GRID_Z
    filt = filt.reshape(BANDS, points)
    applied = applied.reshape(BANDS, points)
    cell_volume = 1.0 / points
    correlation = jnp.dot(filt, filt.T, preferred_element_type=jnp.float32) * cell_volume
    hamil_sub = jnp.dot(filt, applied.T, preferred_element_type=jnp.float32) * cell_volume
    scale = jnp.sqrt(jnp.sum(correlation * correlation) + 1e-06)
    scaled = correlation / scale
    identity = jnp.eye(BANDS, dtype=jnp.float32)
    inverse = identity
    high = lax.Precision.HIGHEST
    for repeat in range(NS_STEPS):
        factor = 1.5 * identity - 0.5 * jnp.dot(inverse, scaled, precision=high)
        scaled = jnp.dot(factor, scaled, precision=high)
        inverse = jnp.dot(factor, inverse, precision=high)
    transform = inverse / jnp.sqrt(scale)
    projected = jnp.dot(jnp.dot(transform.T, hamil_sub, precision=high), transform, precision=high)
    rotated = jnp.dot(transform.T, filt.astype(jnp.float32), precision=high).astype(jnp.bfloat16)
    return (rotated.reshape(BANDS, grid_x, GRID_Y * GRID_Z), projected)
```

```python
import jax
import jax.numpy as jnp
from jax import lax
from jax.experimental import pallas as pl
from jax.experimental.pallas import tpu as pltpu
from jax.sharding import Mesh
from jax.sharding import PartitionSpec as P

f32, bf16 = jnp.float32, jnp.bfloat16

def filter_kernel(bounds_ref, in_ref, out_ref, cur, old, pot):
    lower = bounds_ref[0]
    upper = bounds_ref[1]
    half = (upper - lower) / 2.0
    centre = (upper + lower) / 2.0
    inv = 1.0 / half
    sub = lax.broadcasted_iota(jnp.int32, (8, 2048), 0)
    lane = lax.broadcasted_iota(jnp.int32, (8, 2048), 1)
    first = lax.rem(lane, 32) == 0
    last = lax.rem(lane, 32) == 31
    low = sub < 2
    high = sub >= 6

    @pl.loop(0, 8)
    def _(s):
        both = in_ref[s].astype(f32)
        cur[s] = both[:8]
        pieces = both[8:12] + both[12:16]
        rows = jnp.broadcast_to(pieces[0:1], (8, 2048))
        for x in range(1, 4):
            rows = jnp.where(sub >= 2 * x, jnp.broadcast_to(pieces[x : x + 1], (8, 2048)), rows)
        pot[s] = rows + 3.0

    def neighbours(s, src):
        me = src[s]
        nxt = src[lax.rem(s + 1, 8)]
        prv = src[lax.rem(s + 7, 8)]
        total = pltpu.roll(jnp.where(low, nxt, me), 6, 0) + pltpu.roll(jnp.where(high, prv, me), 2, 0)
        yp = pltpu.roll(me, 2048 - 32, 1)
        ym = pltpu.roll(me, 32, 1)
        total = total + yp + ym
        total = total + pltpu.roll(jnp.where(first, ym, me), 2047, 1)
        total = total + pltpu.roll(jnp.where(last, yp, me), 1, 1)
        return total, me

    @pl.loop(0, 8)
    def _(s):
        total, me = neighbours(s, cur)
        old[s] = (-0.5 * inv) * total + ((pot[s] - centre) * inv) * me

    def step(src, dst):
        @pl.loop(0, 8)
        def _(s):
            total, me = neighbours(s, src)
            dst[s] = (-inv) * total + ((pot[s] - centre) * (2.0 * inv)) * me - dst[s]

    step(old, cur)
    @pl.loop(0, 3)
    def _(k):
        step(cur, old)
        step(old, cur)

    @pl.loop(0, 8)
    def _(s):
        total, me = neighbours(s, cur)
        applied = -0.5 * total + pot[s] * me
        for x in range(4):
            for j in range(8):
                for c in range(1):
                    out_ref[x, j, s, 0:2, :] = me[2 * x : 2 * x + 2, 256 * j : 256 * j + 256].astype(bf16)
                    out_ref[x, j, s, 2:4, :] = applied[2 * x : 2 * x + 2, 256 * j : 256 * j + 256].astype(bf16)

def run_filter(bounds, packed):
    return pl.pallas_call(
        filter_kernel,
        out_shape=jax.ShapeDtypeStruct((4, 8, 8, 4, 256), bf16),
        in_specs=[pl.BlockSpec(memory_space=pltpu.SMEM), pl.BlockSpec(memory_space=pltpu.VMEM)],
        out_specs=pl.BlockSpec(memory_space=pltpu.VMEM),
        scratch_shapes=[pltpu.VMEM((8, 8, 2048), f32)] * 3,
        compiler_params=pltpu.CompilerParams(vmem_limit_bytes=16 << 20),
    )(bounds, packed)

N = 512


def put(ref, x):
    hi = x.astype(bf16)
    ref[0] = hi
    ref[1] = (x - hi.astype(f32)).astype(bf16)


def mm(a, b):
    dot = lambda p, q: jnp.dot(p, q, preferred_element_type=f32)
    return dot(a[0], b[0]) + dot(a[0], b[1]) + dot(a[1], b[0])


def untile(ref, out):
    @pl.loop(0, 32)
    def _(r):
        for c in range(4):
            out[pl.ds(16 * r, 16), 128 * c : 128 * c + 128] = ref[4 * r + c]


def unfold(folded, out, eye):
    mirror = lax.dot_general(eye, folded[...], (((1,), (1,)), ((), ())), preferred_element_type=f32)
    out[...] = mirror + folded[...].astype(f32)
    row = lax.broadcasted_iota(jnp.int32, (128, 128), 0)
    col = lax.broadcasted_iota(jnp.int32, (128, 128), 1)
    spot = (col == row - 1) & (row % 16 > 0) | (row % 16 == 15) & (col == row - 15)
    turned = (row == col - 1) & (col % 16 > 0) | (col % 16 == 15) & (row == col - 15)
    for k in range(0, N, 128):
        here = folded[k : k + 128, k : k + 128].astype(f32)
        there = mirror[k : k + 128, k : k + 128]
        low = jnp.where(row % 16 > 0, pltpu.roll(here, 1, 1), pltpu.roll(there, 113, 1))
        block = jnp.where(spot, there, jnp.where(turned, here, here + there))
        out[k : k + 128, k : k + 128] = jnp.where(row == col, here + low, block)


def ns_kernel(core_ref, mine_ref, other_ref, filt_ref, rot_ref, proj_ref, mat, fold, m, sq, q, g, z, gf):
    core = core_ref[0]
    row = lax.broadcasted_iota(jnp.int32, (N, N), 0)
    col = lax.broadcasted_iota(jnp.int32, (N, N), 1)
    eye = jnp.where(row == col, 1.0, 0.0)

    @pl.when(core == 0)
    def _():
        untile(mine_ref, fold.at[0])
        untile(other_ref, fold.at[1])

    @pl.when(core == 1)
    def _():
        untile(mine_ref, fold.at[1])
        untile(other_ref, fold.at[0])

    unfold(fold.at[0], mat, eye.astype(bf16))
    corr = mat[...]
    scale = jnp.sqrt(jnp.sum(corr * corr) + 1e-6)
    mat[...] = corr / scale
    put(m, mat[...])

    def factor():
        square = mm(m, m)
        put(sq, square)
        put(q, 0.0625 * square - 0.5625 * mat[...])
        gf[...] = 2.25 * eye - 2.4375 * mat[...] + 1.6875 * square
        gf[...] += mm(sq, q)
        put(g, gf[...])

    def advance():
        put(q, mm(g, m))
        mat[...] = mm(g, q)
        put(m, mat[...])

    factor()
    z[...] = g[...]
    advance()

    @pl.loop(0, 2)
    def _(k):
        factor()
        put(z, mm(g, z))
        advance()

    factor()
    put(z, mm(g, z) * lax.rsqrt(scale))
    rot_ref[...] = (
        jnp.dot(z[0], filt_ref[...], preferred_element_type=f32)
        + jnp.dot(z[1], filt_ref[...], preferred_element_type=f32)
    ).astype(bf16)
    unfold(fold.at[1], mat, eye.astype(bf16))
    put(sq, mat[...])
    put(q, mm(sq, z))
    proj_ref[...] = mm(z, q)


def run_ns(core, mine, other, filt):
    v = pl.BlockSpec(memory_space=pltpu.VMEM)
    return pl.pallas_call(
        ns_kernel,
        out_shape=(jax.ShapeDtypeStruct((N, filt.shape[1]), bf16), jax.ShapeDtypeStruct((N, N), f32)),
        in_specs=[pl.BlockSpec(memory_space=pltpu.SMEM), v, v, v],
        out_specs=(v, v),
        scratch_shapes=[pltpu.VMEM((N, N), f32)] + [pltpu.VMEM((2, N, N), bf16)] * 6 + [pltpu.VMEM((N, N), f32)],
        compiler_params=pltpu.CompilerParams(vmem_limit_bytes=32 << 20),
    )(core, mine, other, filt)


def sum_kernel(chip_ref, in_ref, out_ref):
    def add(k, total):
        for step in range(8):
            total = total + in_ref[8 * k + step].astype(f32)
        return total

    total = lax.fori_loop(0, 16, add, jnp.zeros((16, 128), f32))
    chip = chip_ref[0]
    sub = lax.broadcasted_iota(jnp.int32, (16, 128), 0)
    row = sub + 16 * (chip // 4)
    col = lax.broadcasted_iota(jnp.int32, (16, 128), 1) + 128 * (chip % 4)
    hi = total.astype(bf16).astype(f32)
    lo = total - hi
    diagonal = jnp.sum(jnp.where(row == col, lo, 0.0), axis=1, keepdims=True)
    folded = jnp.where(col >= row, hi, lo)
    folded = jnp.where((col == row - 1) & (sub > 0), diagonal, folded)
    folded = jnp.where((sub == 15) & (col == row - 15), diagonal[0:1], folded)
    folded = folded.astype(bf16)

    @pl.loop(0, 16)
    def _(k):
        for step in range(8):
            out_ref[8 * k + step] = folded


def run_sum(chip, parts):
    return pl.pallas_call(
        sum_kernel,
        out_shape=jax.ShapeDtypeStruct((128, 16, 128), bf16),
        in_specs=[pl.BlockSpec(memory_space=pltpu.SMEM), pl.BlockSpec(memory_space=pltpu.VMEM)],
        out_specs=pl.BlockSpec(memory_space=pltpu.VMEM),
    )(chip, parts)

VMEM = pl.BlockSpec(memory_space=pltpu.VMEM)
SMEM = pl.BlockSpec(memory_space=pltpu.SMEM)


def gram_kernel(core_ref, near_ref, far_ref, out_ref, acc):
    dims = (((1,), (1,)), ((), ()))

    def product(right):
        total = lax.dot_general(near_ref[0], near_ref[right], dims, preferred_element_type=f32)
        total += lax.dot_general(far_ref[0], far_ref[right], dims, preferred_element_type=f32)
        acc[...] = total * (1.0 / 65536.0)

    @pl.when(core_ref[0] == 0)
    def _():
        product(0)

    @pl.when(core_ref[0] == 1)
    def _():
        product(1)

    @pl.loop(0, 32)
    def _(r):
        for c in range(4):
            out_ref[4 * r + c] = acc[pl.ds(16 * r, 16), 128 * c : 128 * c + 128].astype(bf16)


def run_gram(core, near, far):
    return pl.pallas_call(
        gram_kernel,
        out_shape=jax.ShapeDtypeStruct((128, 16, 128), bf16),
        in_specs=[SMEM, VMEM, VMEM],
        out_specs=VMEM,
        scratch_shapes=[pltpu.VMEM((N, N), f32)],
        compiler_params=pltpu.CompilerParams(vmem_limit_bytes=16 << 20),
    )(core, near, far)


def exchange(array, axes):
    return lax.all_to_all(array, axes, split_axis=0, concat_axis=0, tiled=True)


def body(orbitals, potential, bounds):
    core = lax.axis_index("core").astype(jnp.int32)[None]
    swap = [(0, 1), (1, 0)]
    chips = ("z", "x", "y")
    bands = orbitals.reshape(8, 2, 4, 2048).transpose(0, 2, 1, 3).reshape(8, 8, 2048)
    coarse = lax.reduce_precision(potential, 8, 7)
    pieces = jnp.concatenate([coarse, potential - coarse]).astype(bf16)
    packed = jnp.concatenate([bands, jnp.broadcast_to(pieces, (8, 8, 2048))], axis=1)
    whole = exchange(packed, ("y", "core"))
    pair = run_filter(bounds, whole).reshape(256, 4, 256)
    pair = exchange(pair, ("z", "x", "y", "core"))
    near = pair.reshape(256, 2, 2, 256).transpose(1, 0, 2, 3).reshape(2, N, 256)
    far = lax.ppermute(near, "core", swap)
    parts = exchange(run_gram(core, near, far), chips)
    chip = lax.axis_index(chips).astype(jnp.int32)[None]
    mine = exchange(run_sum(chip, parts), chips)
    other = lax.ppermute(mine, "core", swap)
    rotated, projected = run_ns(core, mine, other, near[0])
    rotated = exchange(rotated.reshape(32, 16, 256), ("z", "x"))
    rotated = rotated.reshape(4, 8, 16, 256).transpose(2, 0, 1, 3).reshape(16, 4, 2048)
    return rotated, projected


def solution(mesh):
    fine = Mesh(mesh.devices.reshape(8, 4, 4, 2), ("z", "x", "y", "core"))
    return jax.shard_map(
        body,
        mesh=fine,
        in_specs=(P(("z", "x"), ("y", "core"), None), P(("y", "core"), None), P()),
        out_specs=(P(("z", "x"), ("y", "core"), None), P()),
        check_vma=False,
    )
```

```python
import jax
import jax.numpy as jnp
from jax import lax
from jax.experimental import pallas as pl
from jax.experimental.pallas import tpu as pltpu
from jax.sharding import Mesh
from jax.sharding import PartitionSpec as P

f32, bf16 = jnp.float32, jnp.bfloat16
def shuffle_matrix():
    natural = lax.broadcasted_iota(jnp.int32, (512, 512), 0)
    spread = lax.broadcasted_iota(jnp.int32, (512, 512), 1)
    place = (natural // 32 % 4) * 128 + (natural % 32) * 4 + natural // 128
    return jnp.where(spread == place, 1.0, 0.0).astype(bf16)


def filter_kernel(bounds_ref, in_ref, mix_ref, out_ref, cur, old, pot, gain, flat):
    lower = bounds_ref[0]
    upper = bounds_ref[1]
    half = (upper - lower) / 2.0
    centre = (upper + lower) / 2.0
    inv = 1.0 / half
    sub = lax.broadcasted_iota(jnp.int32, (8, 128), 0)
    part = lax.broadcasted_iota(jnp.int32, (8, 128), 1) % 4

    def wrap(ref):
        for k in range(8):
            rows = slice(8 + 8 * k, 16 + 8 * k)
            v = ref[1, rows]
            ref[17, rows] = jnp.where(part < 3, pltpu.roll(v, 127, 1), pltpu.roll(v, 3, 1))
            v = ref[16, rows]
            ref[0, rows] = jnp.where(part > 0, pltpu.roll(v, 1, 1), pltpu.roll(v, 125, 1))

    def edges(ref, t, k, v):
        if k == 0:
            ref[t, 72:74] = v[0:2]
        if k == 7:
            ref[t, 6:8] = v[6:8]

    for b in range(4):
        for a in range(4):
            lanes = slice(128 * (4 * a + b), 128 * (4 * a + b) + 128)
            for s in range(8):
                flat[128 * b + 16 * s : 128 * b + 16 * s + 16, 128 * a : 128 * a + 128] = in_ref[s, :, lanes]

    for b in range(4):
        mixed = jnp.dot(flat[128 * b : 128 * b + 128], mix_ref[...], preferred_element_type=f32)
        for c in range(4):
            t = 4 * b + c
            for s in range(8):
                both = mixed[16 * s : 16 * s + 16, 128 * c : 128 * c + 128]
                cur[t + 1, 8 + 8 * s : 16 + 8 * s] = both[:8]
                edges(cur, t + 1, s, both[:8])
                pieces = both[8:12] + both[12:16]
                rows = jnp.broadcast_to(pieces[0:1], (8, 128))
                for x in range(1, 4):
                    rows = jnp.where(sub >= 2 * x, jnp.broadcast_to(pieces[x : x + 1], (8, 128)), rows)
                rows = rows + 3.0
                pot[t, 8 * s : 8 * s + 8] = rows
                gain[t, 8 * s : 8 * s + 8] = (rows - centre) * (2.0 * inv)
                old[t + 1, 8 + 8 * s : 16 + 8 * s] = jnp.zeros((8, 128), f32)
    wrap(cur)

    def sweep(src, emit):
        @pl.loop(0, 16, unroll=16)
        def _(t):
            for k in range(8):
                r = 8 + 8 * k
                me = src[t + 1, r : r + 8]
                total = src[t + 1, r + 2 : r + 10] + src[t + 1, r - 2 : r + 6]
                total = total + src[t + 2, r : r + 8] + src[t, r : r + 8]
                total = total + pltpu.roll(me, 124, 1) + pltpu.roll(me, 4, 1)
                emit(t, k, total, me)

    def step(src, dst, weight):
        def emit(t, k, total, me):
            r = 8 + 8 * k
            new = weight * (gain[t, 8 * k : 8 * k + 8] * me - inv * total) - dst[t + 1, r : r + 8]
            dst[t + 1, r : r + 8] = new
            edges(dst, t + 1, k, new)

        sweep(src, emit)
        wrap(dst)

    @pl.loop(0, 4)
    def _(k):
        step(cur, old, jnp.where(k == 0, 0.5, 1.0))
        step(old, cur, 1.0)

    def emit(t, k, total, me):
        old[t + 1, 8 + 8 * k : 16 + 8 * k] = pot[t, 8 * k : 8 * k + 8] * me - 0.5 * total

    sweep(cur, emit)

    for half_index, ref in enumerate((cur, old)):
        rows2 = slice(2 * half_index, 2 * half_index + 2)
        for b in range(4):
            for c in range(4):
                flat[64 * b : 64 * b + 64, 128 * c : 128 * c + 128] = ref[4 * b + c + 1, 8:72].astype(bf16)
        for b in range(4):
            plain = lax.dot_general(
                flat[64 * b : 64 * b + 64], mix_ref[...], (((1,), (1,)), ((), ())), preferred_element_type=f32
            )
            for a in range(4):
                n = 4 * a + b
                lanes = slice(128 * (n % 2), 128 * (n % 2) + 128)
                for s in range(8):
                    for x in range(4):
                        r = 8 * s + 2 * x
                        out_ref[x, n // 2, s, rows2, lanes] = plain[r : r + 2, 128 * a : 128 * a + 128].astype(bf16)


def run_filter(bounds, packed):
    return pl.pallas_call(
        filter_kernel,
        out_shape=jax.ShapeDtypeStruct((4, 8, 8, 4, 256), bf16),
        in_specs=[
            pl.BlockSpec(memory_space=pltpu.SMEM),
            pl.BlockSpec(memory_space=pltpu.VMEM),
            pl.BlockSpec(memory_space=pltpu.VMEM),
        ],
        out_specs=pl.BlockSpec(memory_space=pltpu.VMEM),
        scratch_shapes=[pltpu.VMEM((18, 80, 128), f32)] * 2
        + [pltpu.VMEM((16, 64, 128), f32)] * 2
        + [pltpu.VMEM((512, 512), bf16)],
        compiler_params=pltpu.CompilerParams(vmem_limit_bytes=10 << 20),
    )(bounds, packed, shuffle_matrix())

N = 512
VMEM = pl.BlockSpec(memory_space=pltpu.VMEM)
SMEM = pl.BlockSpec(memory_space=pltpu.SMEM)
BLOCKS = [(i, j) for i in range(4) for j in range(i + 1, 4)]


def split(x):
    hi = x.astype(bf16).astype(f32)
    return hi, x - hi


def distance(first):
    row = lax.broadcasted_iota(jnp.int32, (16, 128), 0) + first
    return (lax.broadcasted_iota(jnp.int32, (16, 128), 1) - row) & 127


def fold_pair(x):
    return jnp.concatenate(split(x), axis=0).astype(bf16)


def unfold_pair(v):
    return v[0:8] + v[8:16]


def fold_diagonal(x, apart):
    hi, lo = split(x)
    low = jnp.where(apart == 65, pltpu.roll(lo, 65, 1), pltpu.roll(lo, 64, 1))
    return jnp.where(apart <= 64, hi, low).astype(bf16)


def unfold_diagonal(v, apart):
    low = jnp.where(apart == 0, pltpu.roll(v, 63, 1), pltpu.roll(v, 64, 1))
    return v + jnp.where((apart == 0) | (apart >= 2) & (apart < 64), low, 0.0)


def gram_kernel(core_ref, near_ref, far_ref, out_ref, acc):
    dims = (((1,), (1,)), ((), ()))

    def product(right):
        for rows, cols in ((slice(0, 256), slice(0, N)), (slice(256, N), slice(256, N))):
            total = lax.dot_general(near_ref[0, rows], near_ref[right, cols], dims, preferred_element_type=f32)
            total += lax.dot_general(far_ref[0, rows], far_ref[right, cols], dims, preferred_element_type=f32)
            acc[rows, cols] = total * (1.0 / 65536.0)

    @pl.when(core_ref[0] == 0)
    def _():
        product(0)

    @pl.when(core_ref[0] == 1)
    def _():
        product(1)

    for p, (i, j) in enumerate(BLOCKS):
        for g in range(16):
            out_ref[16 * p + g] = fold_pair(acc[128 * i + 8 * g : 128 * i + 8 * g + 8, 128 * j : 128 * j + 128])
    for i in range(4):
        for g in range(8):
            rows = slice(128 * i + 16 * g, 128 * i + 16 * g + 16)
            out_ref[96 + 8 * i + g] = fold_diagonal(acc[rows, 128 * i : 128 * i + 128], distance(16 * g))


def run_gram(core, near, far):
    return pl.pallas_call(
        gram_kernel,
        out_shape=jax.ShapeDtypeStruct((128, 16, 128), bf16),
        in_specs=[SMEM, VMEM, VMEM],
        out_specs=VMEM,
        scratch_shapes=[pltpu.VMEM((N, N), f32)],
        compiler_params=pltpu.CompilerParams(vmem_limit_bytes=6 << 20),
    )(core, near, far)


def sum_kernel(chip_ref, in_ref, out_ref):
    totals = [in_ref[k].astype(f32) for k in range(4)]
    for k in range(4, 128):
        totals[k % 4] = totals[k % 4] + in_ref[k].astype(f32)
    total = (totals[0] + totals[1]) + (totals[2] + totals[3])
    chip = chip_ref[0]
    apart = distance(16 * (chip % 8))
    pairs = fold_pair(unfold_pair(total)).astype(f32)
    diagonal = fold_diagonal(unfold_diagonal(total, apart), apart).astype(f32)
    folded = jnp.where(chip < 96, pairs, diagonal).astype(bf16)
    for k in range(128):
        out_ref[k] = folded


def run_sum(chip, parts):
    return pl.pallas_call(
        sum_kernel,
        out_shape=jax.ShapeDtypeStruct((128, 16, 128), bf16),
        in_specs=[SMEM, VMEM],
        out_specs=VMEM,
        compiler_params=pltpu.CompilerParams(vmem_limit_bytes=4 << 20),
    )(chip, parts)


def unfold(ref, out):
    for p, (i, j) in enumerate(BLOCKS):
        for g in range(16):
            out[128 * i + 8 * g : 128 * i + 8 * g + 8, 128 * j : 128 * j + 128] = unfold_pair(
                ref[16 * p + g].astype(f32)
            )
        block = out[128 * i : 128 * i + 128, 128 * j : 128 * j + 128]
        out[128 * j : 128 * j + 128, 128 * i : 128 * i + 128] = block.T
    apart = lax.broadcasted_iota(jnp.int32, (128, 128), 1) - lax.broadcasted_iota(jnp.int32, (128, 128), 0)
    apart = apart & 127
    for i in range(4):
        cols = slice(128 * i, 128 * i + 128)
        for g in range(8):
            rows = slice(128 * i + 16 * g, 128 * i + 16 * g + 16)
            out[rows, cols] = unfold_diagonal(ref[96 + 8 * i + g].astype(f32), distance(16 * g))
        block = out[cols, cols]
        out[cols, cols] = jnp.where(apart <= 64, block, block.T)


def put(ref, x):
    hi, lo = split(x)
    ref[0] = hi.astype(bf16)
    ref[1] = lo.astype(bf16)


def dot(a, b):
    return jnp.dot(a, b, preferred_element_type=f32)


def eye():
    return lax.broadcasted_iota(jnp.int32, (N, N), 0) == lax.broadcasted_iota(jnp.int32, (N, N), 1)


def ns_kernel(core_ref, mine_ref, other_ref, filt_ref, rot_ref, trans_ref, m, mb, s, sb, qb, g, gb, n, nb, z, zb):
    halves = (slice(0, 256), slice(256, N))

    @pl.when(core_ref[0] == 0)
    def _():
        unfold(mine_ref, m)

    @pl.when(core_ref[0] == 1)
    def _():
        unfold(other_ref, m)

    corr = m[...]
    scale = jnp.sqrt(jnp.sum(corr * corr) + 1e-6)
    centre = jnp.sum(jnp.where(eye(), corr, 0.0)) / (N * scale)
    m[...] = m[...] / scale - jnp.where(eye(), centre, 0.0)
    mb[...] = m[...].astype(bf16)

    def factor(mu):
        square = mu * mu
        for c in halves:
            s[:, c] = dot(mb[...], mb[:, c]) + (2.0 * mu) * m[:, c]
            sb[:, c] = s[:, c].astype(bf16)
            qb[:, c] = (0.0625 * s[:, c] - 0.5625 * m[:, c]).astype(bf16)
        low = 0.0625 * square - 0.5625 * mu
        for c in halves:
            g[:, c] = (
                dot(sb[...], qb[:, c])
                + (1.6875 + low + 0.0625 * square) * s[:, c]
                - (2.4375 + 0.5625 * square) * m[:, c]
            )
            gb[:, c] = g[:, c].astype(bf16)
        return 2.25 - 2.4375 * mu + 1.6875 * square + square * low

    def advance(mu, gain):
        mid = gain * mu
        for c in halves:
            n[:, c] = dot(gb[...], mb[:, c]) + gain * m[:, c] + mu * g[:, c]
            nb[:, c] = n[:, c].astype(bf16)
        for c in halves:
            m[:, c] = dot(gb[...], nb[:, c]) + gain * n[:, c] + mid * g[:, c]
            mb[:, c] = m[:, c].astype(bf16)
        return gain * mid

    def grow(level, gain):
        for c in halves:
            z[:, c] = dot(gb[...], zb[:, c]) + gain * z[:, c] + level * g[:, c]
            zb[:, c] = z[:, c].astype(bf16)
        return level * gain

    level = factor(centre)
    z[...] = g[...]
    zb[...] = gb[...]
    mu = advance(centre, level)

    def pair(_, carry):
        mu, level = carry
        gain = factor(mu)
        level = grow(level, gain)
        return advance(mu, gain), level

    mu, level = lax.fori_loop(0, 2, pair, (mu, level))
    level = grow(level, factor(mu))
    shrink = lax.rsqrt(scale)
    put(trans_ref, z[...] * shrink + jnp.where(eye(), level * shrink, 0.0))
    rot_ref[...] = (dot(trans_ref[0], filt_ref[...]) + dot(trans_ref[1], filt_ref[...])).astype(bf16)


def run_ns(core, mine, other, filt):
    wide, narrow = pltpu.VMEM((N, N), f32), pltpu.VMEM((N, N), bf16)
    return pl.pallas_call(
        ns_kernel,
        out_shape=(jax.ShapeDtypeStruct(filt.shape, bf16), jax.ShapeDtypeStruct((2, N, N), bf16)),
        in_specs=[SMEM, VMEM, VMEM, VMEM],
        out_specs=(VMEM, VMEM),
        scratch_shapes=[wide, narrow, wide, narrow, narrow, wide, narrow, wide, narrow, wide, narrow],
        compiler_params=pltpu.CompilerParams(vmem_limit_bytes=20 << 20),
    )(core, mine, other, filt)


def project_kernel(core_ref, mine_ref, other_ref, trans_ref, out_ref, h, w):
    def product(a, b):
        return dot(a[0], b[0]) + dot(a[0], b[1]) + dot(a[1], b[0])

    @pl.when(core_ref[0] == 0)
    def _():
        unfold(other_ref, out_ref)

    @pl.when(core_ref[0] == 1)
    def _():
        unfold(mine_ref, out_ref)

    put(h, out_ref[...])
    put(w, product(h, trans_ref))
    out_ref[...] = product(trans_ref, w)


def run_project(core, mine, other, trans):
    return pl.pallas_call(
        project_kernel,
        out_shape=jax.ShapeDtypeStruct((N, N), f32),
        in_specs=[SMEM, VMEM, VMEM, VMEM],
        out_specs=VMEM,
        scratch_shapes=[pltpu.VMEM((2, N, N), bf16)] * 2,
        compiler_params=pltpu.CompilerParams(vmem_limit_bytes=10 << 20),
        cost_estimate=pl.CostEstimate(flops=12 * N**3, bytes_accessed=4 * N * N, transcendentals=0),
    )(core, mine, other, trans)

def exchange(array, axes):
    return lax.all_to_all(array, axes, split_axis=0, concat_axis=0, tiled=True)


def body(orbitals, potential, bounds):
    core = lax.axis_index("core").astype(jnp.int32)[None]
    swap = [(0, 1), (1, 0)]
    chips = ("z", "x", "y")
    chip = lax.axis_index(chips).astype(jnp.int32)[None]
    bands = orbitals.reshape(8, 2, 4, 2048).transpose(0, 2, 1, 3).reshape(8, 8, 2048)
    coarse = lax.reduce_precision(potential, 8, 7)
    pieces = jnp.concatenate([coarse, potential - coarse]).astype(bf16)
    packed = jnp.concatenate([bands, jnp.broadcast_to(pieces, (8, 8, 2048))], axis=1)
    whole = exchange(packed, ("y", "core"))
    pair = run_filter(bounds, whole).reshape(256, 4, 256)
    pair = exchange(pair, ("z", "x", "y", "core"))
    near = pair.reshape(256, 2, 2, 256).transpose(1, 0, 2, 3).reshape(2, N, 256)
    far = lax.ppermute(near, "core", swap)
    parts = exchange(run_gram(core, near, far), chips)
    mine = exchange(run_sum(chip, parts), chips)
    other = lax.ppermute(mine, "core", swap)
    rotated, transform = run_ns(core, mine, other, near[0])
    projected = run_project(core, mine, other, transform)
    rotated = exchange(rotated.reshape(32, 16, 256), ("z", "x"))
    rotated = rotated.reshape(4, 8, 16, 256).transpose(2, 0, 1, 3).reshape(16, 4, 2048)
    return rotated, projected


def solution(mesh):
    fine = Mesh(mesh.devices.reshape(8, 4, 4, 2), ("z", "x", "y", "core"))
    return jax.shard_map(
        body,
        mesh=fine,
        in_specs=(P(("z", "x"), ("y", "core"), None), P(("y", "core"), None), P()),
        out_specs=(P(("z", "x"), ("y", "core"), None), P()),
        check_vma=False,
    )
```

```python
import jax
import jax.numpy as jnp
from jax import lax
from jax.experimental import pallas as pl
from jax.experimental.pallas import tpu as pltpu
from jax.sharding import Mesh
from jax.sharding import PartitionSpec as P

f32, bf16 = jnp.float32, jnp.bfloat16
def shuffle_matrix():
    natural = lax.broadcasted_iota(jnp.int32, (512, 512), 0)
    spread = lax.broadcasted_iota(jnp.int32, (512, 512), 1)
    place = (natural // 32 % 4) * 128 + (natural % 32) * 4 + natural // 128
    return jnp.where(spread == place, 1.0, 0.0).astype(bf16)


def filter_kernel(bounds_ref, in_ref, mix_ref, out_ref, cur, old, pot, gain, flat):
    lower = bounds_ref[0]
    upper = bounds_ref[1]
    half = (upper - lower) / 2.0
    centre = (upper + lower) / 2.0
    inv = 1.0 / half
    sub = lax.broadcasted_iota(jnp.int32, (8, 128), 0)
    part = lax.broadcasted_iota(jnp.int32, (8, 128), 1) % 4

    def wrap(ref):
        for k in range(8):
            rows = slice(8 + 8 * k, 16 + 8 * k)
            v = ref[1, rows]
            ref[17, rows] = jnp.where(part < 3, pltpu.roll(v, 127, 1), pltpu.roll(v, 3, 1))
            v = ref[16, rows]
            ref[0, rows] = jnp.where(part > 0, pltpu.roll(v, 1, 1), pltpu.roll(v, 125, 1))

    def edges(ref, t, k, v):
        if k == 0:
            ref[t, 72:74] = v[0:2]
        if k == 7:
            ref[t, 6:8] = v[6:8]

    for b in range(4):
        for a in range(4):
            lanes = slice(128 * (4 * a + b), 128 * (4 * a + b) + 128)
            for s in range(8):
                flat[128 * b + 16 * s : 128 * b + 16 * s + 16, 128 * a : 128 * a + 128] = in_ref[s, :, lanes]

    for b in range(4):
        mixed = jnp.dot(flat[128 * b : 128 * b + 128], mix_ref[...], preferred_element_type=f32)
        for c in range(4):
            t = 4 * b + c
            for s in range(8):
                both = mixed[16 * s : 16 * s + 16, 128 * c : 128 * c + 128]
                cur[t + 1, 8 + 8 * s : 16 + 8 * s] = both[:8]
                edges(cur, t + 1, s, both[:8])
                pieces = both[8:12] + both[12:16]
                rows = jnp.broadcast_to(pieces[0:1], (8, 128))
                for x in range(1, 4):
                    rows = jnp.where(sub >= 2 * x, jnp.broadcast_to(pieces[x : x + 1], (8, 128)), rows)
                rows = rows + 3.0
                pot[t, 8 * s : 8 * s + 8] = rows
                gain[t, 8 * s : 8 * s + 8] = (rows - centre) * (2.0 * inv)
                old[t + 1, 8 + 8 * s : 16 + 8 * s] = jnp.zeros((8, 128), f32)
    wrap(cur)

    def sweep(src, emit):
        @pl.loop(0, 16, unroll=16)
        def _(t):
            for k in range(8):
                r = 8 + 8 * k
                me = src[t + 1, r : r + 8]
                total = src[t + 1, r + 2 : r + 10] + src[t + 1, r - 2 : r + 6]
                total = total + src[t + 2, r : r + 8] + src[t, r : r + 8]
                total = total + pltpu.roll(me, 124, 1) + pltpu.roll(me, 4, 1)
                emit(t, k, total, me)

    def step(src, dst, weight):
        def emit(t, k, total, me):
            r = 8 + 8 * k
            new = weight * (gain[t, 8 * k : 8 * k + 8] * me - inv * total) - dst[t + 1, r : r + 8]
            dst[t + 1, r : r + 8] = new
            edges(dst, t + 1, k, new)

        sweep(src, emit)
        wrap(dst)

    @pl.loop(0, 4)
    def _(k):
        step(cur, old, jnp.where(k == 0, 0.5, 1.0))
        step(old, cur, 1.0)

    def emit(t, k, total, me):
        old[t + 1, 8 + 8 * k : 16 + 8 * k] = pot[t, 8 * k : 8 * k + 8] * me - 0.5 * total

    sweep(cur, emit)

    for half_index, ref in enumerate((cur, old)):
        rows2 = slice(2 * half_index, 2 * half_index + 2)
        for b in range(4):
            for c in range(4):
                flat[64 * b : 64 * b + 64, 128 * c : 128 * c + 128] = ref[4 * b + c + 1, 8:72].astype(bf16)
        for b in range(4):
            plain = lax.dot_general(
                flat[64 * b : 64 * b + 64], mix_ref[...], (((1,), (1,)), ((), ())), preferred_element_type=f32
            )
            for a in range(4):
                n = 4 * a + b
                lanes = slice(128 * (n % 2), 128 * (n % 2) + 128)
                for s in range(8):
                    for x in range(4):
                        r = 8 * s + 2 * x
                        out_ref[x, n // 2, s, rows2, lanes] = plain[r : r + 2, 128 * a : 128 * a + 128].astype(bf16)


def run_filter(bounds, packed):
    return pl.pallas_call(
        filter_kernel,
        out_shape=jax.ShapeDtypeStruct((4, 8, 8, 4, 256), bf16),
        in_specs=[
            pl.BlockSpec(memory_space=pltpu.SMEM),
            pl.BlockSpec(memory_space=pltpu.VMEM),
            pl.BlockSpec(memory_space=pltpu.VMEM),
        ],
        out_specs=pl.BlockSpec(memory_space=pltpu.VMEM),
        scratch_shapes=[pltpu.VMEM((18, 80, 128), f32)] * 2
        + [pltpu.VMEM((16, 64, 128), f32)] * 2
        + [pltpu.VMEM((512, 512), bf16)],
        compiler_params=pltpu.CompilerParams(vmem_limit_bytes=10 << 20),
    )(bounds, packed, shuffle_matrix())

N = 512
VMEM = pl.BlockSpec(memory_space=pltpu.VMEM)
SMEM = pl.BlockSpec(memory_space=pltpu.SMEM)
BLOCKS = [(i, j) for i in range(4) for j in range(i + 1, 4)]


def split(x):
    hi = x.astype(bf16).astype(f32)
    return hi, x - hi


def distance(first):
    row = lax.broadcasted_iota(jnp.int32, (16, 128), 0) + first
    return (lax.broadcasted_iota(jnp.int32, (16, 128), 1) - row) & 127


def fold_pair(x):
    return jnp.concatenate(split(x), axis=0).astype(bf16)


def unfold_pair(v):
    return v[0:8] + v[8:16]


def fold_diagonal(x, apart):
    hi, lo = split(x)
    low = jnp.where(apart == 65, pltpu.roll(lo, 65, 1), pltpu.roll(lo, 64, 1))
    return jnp.where(apart <= 64, hi, low).astype(bf16)


def unfold_diagonal(v, apart):
    low = jnp.where(apart == 0, pltpu.roll(v, 63, 1), pltpu.roll(v, 64, 1))
    return v + jnp.where((apart == 0) | (apart >= 2) & (apart < 64), low, 0.0)


def gram_kernel(core_ref, near_ref, far_ref, out_ref, acc):
    dims = (((1,), (1,)), ((), ()))

    def product(right):
        for rows, cols in ((slice(0, 256), slice(0, N)), (slice(256, N), slice(256, N))):
            total = lax.dot_general(near_ref[0, rows], near_ref[right, cols], dims, preferred_element_type=f32)
            total += lax.dot_general(far_ref[0, rows], far_ref[right, cols], dims, preferred_element_type=f32)
            acc[rows, cols] = total * (1.0 / 65536.0)

    @pl.when(core_ref[0] == 0)
    def _():
        product(0)

    @pl.when(core_ref[0] == 1)
    def _():
        product(1)

    for p, (i, j) in enumerate(BLOCKS):
        for g in range(16):
            out_ref[16 * p + g] = fold_pair(acc[128 * i + 8 * g : 128 * i + 8 * g + 8, 128 * j : 128 * j + 128])
    for i in range(4):
        for g in range(8):
            rows = slice(128 * i + 16 * g, 128 * i + 16 * g + 16)
            out_ref[96 + 8 * i + g] = fold_diagonal(acc[rows, 128 * i : 128 * i + 128], distance(16 * g))


def run_gram(core, near, far):
    return pl.pallas_call(
        gram_kernel,
        out_shape=jax.ShapeDtypeStruct((128, 16, 128), bf16),
        in_specs=[SMEM, VMEM, VMEM],
        out_specs=VMEM,
        scratch_shapes=[pltpu.VMEM((N, N), f32)],
        compiler_params=pltpu.CompilerParams(vmem_limit_bytes=6 << 20),
    )(core, near, far)


def sum_kernel(chip_ref, in_ref, out_ref):
    chip = chip_ref[0]
    for u in range(8):
        total = in_ref[0, u].astype(f32)
        for k in range(1, in_ref.shape[0]):
            total = total + in_ref[k, u].astype(f32)
        apart = distance(16 * u)
        pairs = fold_pair(unfold_pair(total)).astype(f32)
        diagonal = fold_diagonal(unfold_diagonal(total, apart), apart).astype(f32)
        folded = jnp.where(chip < 12, pairs, diagonal).astype(bf16)
        for k in range(out_ref.shape[0]):
            out_ref[k, u] = folded


def run_sum(chip, parts, copies):
    return pl.pallas_call(
        sum_kernel,
        out_shape=jax.ShapeDtypeStruct((copies, 8, 16, 128), bf16),
        in_specs=[SMEM, VMEM],
        out_specs=VMEM,
        compiler_params=pltpu.CompilerParams(vmem_limit_bytes=4 << 20),
    )(chip, parts)


def unfold(ref, out):
    for p, (i, j) in enumerate(BLOCKS):
        for g in range(16):
            out[128 * i + 8 * g : 128 * i + 8 * g + 8, 128 * j : 128 * j + 128] = unfold_pair(
                ref[16 * p + g].astype(f32)
            )
        block = out[128 * i : 128 * i + 128, 128 * j : 128 * j + 128]
        out[128 * j : 128 * j + 128, 128 * i : 128 * i + 128] = block.T
    apart = lax.broadcasted_iota(jnp.int32, (128, 128), 1) - lax.broadcasted_iota(jnp.int32, (128, 128), 0)
    apart = apart & 127
    for i in range(4):
        cols = slice(128 * i, 128 * i + 128)
        for g in range(8):
            rows = slice(128 * i + 16 * g, 128 * i + 16 * g + 16)
            out[rows, cols] = unfold_diagonal(ref[96 + 8 * i + g].astype(f32), distance(16 * g))
        block = out[cols, cols]
        out[cols, cols] = jnp.where(apart <= 64, block, block.T)


def put(ref, x):
    hi, lo = split(x)
    ref[0] = hi.astype(bf16)
    ref[1] = lo.astype(bf16)


def dot(a, b):
    return jnp.dot(a, b, preferred_element_type=f32)


def eye():
    return lax.broadcasted_iota(jnp.int32, (N, N), 0) == lax.broadcasted_iota(jnp.int32, (N, N), 1)


def ns_kernel(core_ref, mine_ref, other_ref, filt_ref, rot_ref, trans_ref, m, mb, s, sb, qb, g, gb, n, nb, z, zb):
    halves = (slice(0, 256), slice(256, N))

    @pl.when(core_ref[0] == 0)
    def _():
        unfold(mine_ref, m)

    @pl.when(core_ref[0] == 1)
    def _():
        unfold(other_ref, m)

    corr = m[...]
    scale = jnp.sqrt(jnp.sum(corr * corr) + 1e-6)
    centre = jnp.sum(jnp.where(eye(), corr, 0.0)) / (N * scale)
    m[...] = m[...] / scale - jnp.where(eye(), centre, 0.0)
    mb[...] = m[...].astype(bf16)

    def factor(mu):
        square = mu * mu
        for c in halves:
            s[:, c] = dot(mb[...], mb[:, c]) + (2.0 * mu) * m[:, c]
            sb[:, c] = s[:, c].astype(bf16)
            qb[:, c] = (0.0625 * s[:, c] - 0.5625 * m[:, c]).astype(bf16)
        low = 0.0625 * square - 0.5625 * mu
        for c in halves:
            g[:, c] = (
                dot(sb[...], qb[:, c])
                + (1.6875 + low + 0.0625 * square) * s[:, c]
                - (2.4375 + 0.5625 * square) * m[:, c]
            )
            gb[:, c] = g[:, c].astype(bf16)
        return 2.25 - 2.4375 * mu + 1.6875 * square + square * low

    def advance(mu, gain):
        mid = gain * mu
        for c in halves:
            n[:, c] = dot(gb[...], mb[:, c]) + gain * m[:, c] + mu * g[:, c]
            nb[:, c] = n[:, c].astype(bf16)
        for c in halves:
            m[:, c] = dot(gb[...], nb[:, c]) + gain * n[:, c] + mid * g[:, c]
            mb[:, c] = m[:, c].astype(bf16)
        return gain * mid

    def grow(level, gain):
        for c in halves:
            z[:, c] = dot(gb[...], zb[:, c]) + gain * z[:, c] + level * g[:, c]
            zb[:, c] = z[:, c].astype(bf16)
        return level * gain

    level = factor(centre)
    z[...] = g[...]
    zb[...] = gb[...]
    mu = advance(centre, level)

    def pair(_, carry):
        mu, level = carry
        gain = factor(mu)
        level = grow(level, gain)
        return advance(mu, gain), level

    mu, level = lax.fori_loop(0, 2, pair, (mu, level))
    level = grow(level, factor(mu))
    shrink = lax.rsqrt(scale)
    put(trans_ref, z[...] * shrink + jnp.where(eye(), level * shrink, 0.0))
    rot_ref[...] = (dot(trans_ref[0], filt_ref[...]) + dot(trans_ref[1], filt_ref[...])).astype(bf16)


def run_ns(core, mine, other, filt):
    wide, narrow = pltpu.VMEM((N, N), f32), pltpu.VMEM((N, N), bf16)
    return pl.pallas_call(
        ns_kernel,
        out_shape=(jax.ShapeDtypeStruct(filt.shape, bf16), jax.ShapeDtypeStruct((2, N, N), bf16)),
        in_specs=[SMEM, VMEM, VMEM, VMEM],
        out_specs=(VMEM, VMEM),
        scratch_shapes=[wide, narrow, wide, narrow, narrow, wide, narrow, wide, narrow, wide, narrow],
        compiler_params=pltpu.CompilerParams(vmem_limit_bytes=20 << 20),
    )(core, mine, other, filt)


def project_kernel(core_ref, mine_ref, other_ref, trans_ref, out_ref, h, w):
    def product(a, b):
        return dot(a[0], b[0]) + dot(a[0], b[1]) + dot(a[1], b[0])

    @pl.when(core_ref[0] == 0)
    def _():
        unfold(other_ref, out_ref)

    @pl.when(core_ref[0] == 1)
    def _():
        unfold(mine_ref, out_ref)

    put(h, out_ref[...])
    put(w, product(h, trans_ref))
    out_ref[...] = product(trans_ref, w)


def run_project(core, mine, other, trans):
    return pl.pallas_call(
        project_kernel,
        out_shape=jax.ShapeDtypeStruct((N, N), f32),
        in_specs=[SMEM, VMEM, VMEM, VMEM],
        out_specs=VMEM,
        scratch_shapes=[pltpu.VMEM((2, N, N), bf16)] * 2,
        compiler_params=pltpu.CompilerParams(vmem_limit_bytes=10 << 20),
        cost_estimate=pl.CostEstimate(flops=12 * N**3, bytes_accessed=4 * N * N, transcendentals=0),
    )(core, mine, other, trans)

def exchange(array, axes):
    return lax.all_to_all(array, axes, split_axis=0, concat_axis=0, tiled=True)


def body(orbitals, potential, bounds):
    core = lax.axis_index("core").astype(jnp.int32)[None]
    swap = [(0, 1), (1, 0)]
    plane = ("x", "y")
    chip = lax.axis_index(plane).astype(jnp.int32)[None]
    bands = orbitals.reshape(8, 2, 4, 2048).transpose(0, 2, 1, 3).reshape(8, 8, 2048)
    coarse = lax.reduce_precision(potential, 8, 7)
    pieces = jnp.concatenate([coarse, potential - coarse]).astype(bf16)
    packed = jnp.concatenate([bands, jnp.broadcast_to(pieces, (8, 8, 2048))], axis=1)
    whole = exchange(packed, ("y", "core"))
    pair = run_filter(bounds, whole).reshape(256, 4, 256)
    pair = exchange(pair, ("z", "x", "y", "core"))
    near = pair.reshape(256, 2, 2, 256).transpose(1, 0, 2, 3).reshape(2, N, 256)
    far = lax.ppermute(near, "core", swap)
    parts = exchange(run_gram(core, near, far).reshape(16, 8, 16, 128), plane)
    parts = exchange(run_sum(chip, parts, 8), "z")
    mine = exchange(run_sum(chip, parts, 16), plane).reshape(128, 16, 128)
    other = lax.ppermute(mine, "core", swap)
    rotated, transform = run_ns(core, mine, other, near[0])
    projected = run_project(core, mine, other, transform)
    rotated = exchange(rotated.reshape(32, 16, 256), ("z", "x"))
    rotated = rotated.reshape(4, 8, 16, 256).transpose(2, 0, 1, 3).reshape(16, 4, 2048)
    return rotated, projected


def solution(mesh):
    fine = Mesh(mesh.devices.reshape(8, 4, 4, 2), ("z", "x", "y", "core"))
    return jax.shard_map(
        body,
        mesh=fine,
        in_specs=(P(("z", "x"), ("y", "core"), None), P(("y", "core"), None), P()),
        out_specs=(P(("z", "x"), ("y", "core"), None), P()),
        check_vma=False,
    )
```

```python
import jax
import jax.numpy as jnp
from jax import lax
from jax.experimental import pallas as pl
from jax.experimental.pallas import tpu as pltpu
from jax.sharding import Mesh
from jax.sharding import PartitionSpec as P

f32, bf16 = jnp.float32, jnp.bfloat16
def shuffle_matrix():
    natural = lax.broadcasted_iota(jnp.int32, (512, 512), 0)
    spread = lax.broadcasted_iota(jnp.int32, (512, 512), 1)
    place = (natural // 32 % 4) * 128 + (natural % 32) * 4 + natural // 128
    return jnp.where(spread == place, 1.0, 0.0).astype(bf16)


def filter_kernel(bounds_ref, in_ref, mix_ref, out_ref, cur, old, pot, gain, flat):
    lower = bounds_ref[0]
    upper = bounds_ref[1]
    half = (upper - lower) / 2.0
    centre = (upper + lower) / 2.0
    inv = 1.0 / half
    sub = lax.broadcasted_iota(jnp.int32, (8, 128), 0)
    part = lax.broadcasted_iota(jnp.int32, (8, 128), 1) % 4

    def wrap(ref):
        for k in range(8):
            rows = slice(8 + 8 * k, 16 + 8 * k)
            v = ref[1, rows]
            ref[17, rows] = jnp.where(part < 3, pltpu.roll(v, 127, 1), pltpu.roll(v, 3, 1))
            v = ref[16, rows]
            ref[0, rows] = jnp.where(part > 0, pltpu.roll(v, 1, 1), pltpu.roll(v, 125, 1))

    def edges(ref, t, k, v):
        if k == 0:
            ref[t, 72:74] = v[0:2]
        if k == 7:
            ref[t, 6:8] = v[6:8]

    for b in range(4):
        for a in range(4):
            lanes = slice(128 * (4 * a + b), 128 * (4 * a + b) + 128)
            for s in range(8):
                flat[128 * b + 16 * s : 128 * b + 16 * s + 16, 128 * a : 128 * a + 128] = in_ref[s, :, lanes]

    for b in range(4):
        mixed = jnp.dot(flat[128 * b : 128 * b + 128], mix_ref[...], preferred_element_type=f32)
        for c in range(4):
            t = 4 * b + c
            for s in range(8):
                both = mixed[16 * s : 16 * s + 16, 128 * c : 128 * c + 128]
                cur[t + 1, 8 + 8 * s : 16 + 8 * s] = both[:8]
                edges(cur, t + 1, s, both[:8])
                pieces = both[8:12] + both[12:16]
                rows = jnp.broadcast_to(pieces[0:1], (8, 128))
                for x in range(1, 4):
                    rows = jnp.where(sub >= 2 * x, jnp.broadcast_to(pieces[x : x + 1], (8, 128)), rows)
                rows = rows + 3.0
                pot[t, 8 * s : 8 * s + 8] = rows
                gain[t, 8 * s : 8 * s + 8] = (rows - centre) * (2.0 * inv)
                old[t + 1, 8 + 8 * s : 16 + 8 * s] = jnp.zeros((8, 128), f32)
    wrap(cur)

    def sweep(src, emit):
        @pl.loop(0, 16, unroll=16)
        def _(t):
            for k in range(8):
                r = 8 + 8 * k
                me = src[t + 1, r : r + 8]
                total = src[t + 1, r + 2 : r + 10] + src[t + 1, r - 2 : r + 6]
                total = total + src[t + 2, r : r + 8] + src[t, r : r + 8]
                total = total + pltpu.roll(me, 124, 1) + pltpu.roll(me, 4, 1)
                emit(t, k, total, me)

    def step(src, dst, weight):
        def emit(t, k, total, me):
            r = 8 + 8 * k
            new = weight * (gain[t, 8 * k : 8 * k + 8] * me - inv * total) - dst[t + 1, r : r + 8]
            dst[t + 1, r : r + 8] = new
            edges(dst, t + 1, k, new)

        sweep(src, emit)
        wrap(dst)

    @pl.loop(0, 4)
    def _(k):
        step(cur, old, jnp.where(k == 0, 0.5, 1.0))
        step(old, cur, 1.0)

    def emit(t, k, total, me):
        old[t + 1, 8 + 8 * k : 16 + 8 * k] = pot[t, 8 * k : 8 * k + 8] * me - 0.5 * total

    sweep(cur, emit)

    for half_index, ref in enumerate((cur, old)):
        rows2 = slice(2 * half_index, 2 * half_index + 2)
        for b in range(4):
            for c in range(4):
                flat[64 * b : 64 * b + 64, 128 * c : 128 * c + 128] = ref[4 * b + c + 1, 8:72].astype(bf16)
        for b in range(4):
            plain = lax.dot_general(
                flat[64 * b : 64 * b + 64], mix_ref[...], (((1,), (1,)), ((), ())), preferred_element_type=f32
            )
            for a in range(4):
                n = 4 * a + b
                lanes = slice(128 * (n % 2), 128 * (n % 2) + 128)
                for s in range(8):
                    for x in range(4):
                        r = 8 * s + 2 * x
                        out_ref[x, n // 2, s, rows2, lanes] = plain[r : r + 2, 128 * a : 128 * a + 128].astype(bf16)


def run_filter(bounds, packed):
    return pl.pallas_call(
        filter_kernel,
        out_shape=jax.ShapeDtypeStruct((4, 8, 8, 4, 256), bf16),
        in_specs=[
            pl.BlockSpec(memory_space=pltpu.SMEM),
            pl.BlockSpec(memory_space=pltpu.VMEM),
            pl.BlockSpec(memory_space=pltpu.VMEM),
        ],
        out_specs=pl.BlockSpec(memory_space=pltpu.VMEM),
        scratch_shapes=[pltpu.VMEM((18, 80, 128), f32)] * 2
        + [pltpu.VMEM((16, 64, 128), f32)] * 2
        + [pltpu.VMEM((512, 512), bf16)],
        compiler_params=pltpu.CompilerParams(vmem_limit_bytes=10 << 20),
    )(bounds, packed, shuffle_matrix())

N = 512
VMEM = pl.BlockSpec(memory_space=pltpu.VMEM)
SMEM = pl.BlockSpec(memory_space=pltpu.SMEM)
BLOCKS = [(i, j) for i in range(4) for j in range(i + 1, 4)]


def split(x):
    hi = x.astype(bf16).astype(f32)
    return hi, x - hi


def distance(first):
    row = lax.broadcasted_iota(jnp.int32, (16, 128), 0) + first
    return (lax.broadcasted_iota(jnp.int32, (16, 128), 1) - row) & 127


def fold_pair(x):
    return jnp.concatenate(split(x), axis=0).astype(bf16)


def unfold_pair(v):
    return v[0:8] + v[8:16]


def fold_diagonal(x, apart):
    hi, lo = split(x)
    low = jnp.where(apart == 65, pltpu.roll(lo, 65, 1), pltpu.roll(lo, 64, 1))
    return jnp.where(apart <= 64, hi, low).astype(bf16)


def unfold_diagonal(v, apart):
    low = jnp.where(apart == 0, pltpu.roll(v, 63, 1), pltpu.roll(v, 64, 1))
    return v + jnp.where((apart == 0) | (apart >= 2) & (apart < 64), low, 0.0)


def gram_kernel(core_ref, near_ref, far_ref, out_ref, acc):
    dims = (((1,), (1,)), ((), ()))

    def product(right):
        for rows, cols in ((slice(0, 256), slice(0, N)), (slice(256, N), slice(256, N))):
            total = lax.dot_general(near_ref[0, rows], near_ref[right, cols], dims, preferred_element_type=f32)
            total += lax.dot_general(far_ref[0, rows], far_ref[right, cols], dims, preferred_element_type=f32)
            acc[rows, cols] = total * (1.0 / 65536.0)

    @pl.when(core_ref[0] == 0)
    def _():
        product(0)

    @pl.when(core_ref[0] == 1)
    def _():
        product(1)

    for p, (i, j) in enumerate(BLOCKS):
        for g in range(16):
            out_ref[16 * p + g] = fold_pair(acc[128 * i + 8 * g : 128 * i + 8 * g + 8, 128 * j : 128 * j + 128])
    for i in range(4):
        for g in range(8):
            rows = slice(128 * i + 16 * g, 128 * i + 16 * g + 16)
            out_ref[96 + 8 * i + g] = fold_diagonal(acc[rows, 128 * i : 128 * i + 128], distance(16 * g))


def run_gram(core, near, far):
    return pl.pallas_call(
        gram_kernel,
        out_shape=jax.ShapeDtypeStruct((128, 16, 128), bf16),
        in_specs=[SMEM, VMEM, VMEM],
        out_specs=VMEM,
        scratch_shapes=[pltpu.VMEM((N, N), f32)],
        compiler_params=pltpu.CompilerParams(vmem_limit_bytes=6 << 20),
    )(core, near, far)


def sum_kernel(chip_ref, in_ref, out_ref):
    chip = chip_ref[0]
    for u in range(8):
        total = in_ref[0, u].astype(f32)
        for k in range(1, in_ref.shape[0]):
            total = total + in_ref[k, u].astype(f32)
        apart = distance(16 * u)
        pairs = fold_pair(unfold_pair(total)).astype(f32)
        diagonal = fold_diagonal(unfold_diagonal(total, apart), apart).astype(f32)
        folded = jnp.where(chip < 12, pairs, diagonal).astype(bf16)
        for k in range(out_ref.shape[0]):
            out_ref[k, u] = folded


def run_sum(chip, parts, copies):
    return pl.pallas_call(
        sum_kernel,
        out_shape=jax.ShapeDtypeStruct((copies, 8, 16, 128), bf16),
        in_specs=[SMEM, VMEM],
        out_specs=VMEM,
        compiler_params=pltpu.CompilerParams(vmem_limit_bytes=4 << 20),
    )(chip, parts)


def unfold(ref, out):
    for p, (i, j) in enumerate(BLOCKS):
        for g in range(16):
            out[128 * i + 8 * g : 128 * i + 8 * g + 8, 128 * j : 128 * j + 128] = unfold_pair(
                ref[16 * p + g].astype(f32)
            )
        block = out[128 * i : 128 * i + 128, 128 * j : 128 * j + 128]
        out[128 * j : 128 * j + 128, 128 * i : 128 * i + 128] = block.T
    apart = lax.broadcasted_iota(jnp.int32, (128, 128), 1) - lax.broadcasted_iota(jnp.int32, (128, 128), 0)
    apart = apart & 127
    for i in range(4):
        cols = slice(128 * i, 128 * i + 128)
        for g in range(8):
            rows = slice(128 * i + 16 * g, 128 * i + 16 * g + 16)
            out[rows, cols] = unfold_diagonal(ref[96 + 8 * i + g].astype(f32), distance(16 * g))
        block = out[cols, cols]
        out[cols, cols] = jnp.where(apart <= 64, block, block.T)


def put(ref, x):
    hi, lo = split(x)
    ref[0] = hi.astype(bf16)
    ref[1] = lo.astype(bf16)


def dot(a, b):
    return jnp.dot(a, b, preferred_element_type=f32)


def eye():
    return lax.broadcasted_iota(jnp.int32, (N, N), 0) == lax.broadcasted_iota(jnp.int32, (N, N), 1)


def ns_kernel(core_ref, mine_ref, other_ref, trans_ref, m, mb, s, sb, qb, g, gb, n, nb, z, zb):
    halves = (slice(0, 256), slice(256, N))

    @pl.when(core_ref[0] == 0)
    def _():
        unfold(mine_ref, m)

    @pl.when(core_ref[0] == 1)
    def _():
        unfold(other_ref, m)

    corr = m[...]
    scale = jnp.sqrt(jnp.sum(corr * corr) + 1e-6)
    centre = jnp.sum(jnp.where(eye(), corr, 0.0)) / (N * scale)
    m[...] = m[...] / scale - jnp.where(eye(), centre, 0.0)
    mb[...] = m[...].astype(bf16)

    def factor(mu):
        square = mu * mu
        for c in halves:
            s[:, c] = dot(mb[...], mb[:, c]) + (2.0 * mu) * m[:, c]
            sb[:, c] = s[:, c].astype(bf16)
            qb[:, c] = (0.0625 * s[:, c] - 0.5625 * m[:, c]).astype(bf16)
        low = 0.0625 * square - 0.5625 * mu
        for c in halves:
            g[:, c] = (
                dot(sb[...], qb[:, c])
                + (1.6875 + low + 0.0625 * square) * s[:, c]
                - (2.4375 + 0.5625 * square) * m[:, c]
            )
            gb[:, c] = g[:, c].astype(bf16)
        return 2.25 - 2.4375 * mu + 1.6875 * square + square * low

    def advance(mu, gain):
        mid = gain * mu
        for c in halves:
            n[:, c] = dot(gb[...], mb[:, c]) + gain * m[:, c] + mu * g[:, c]
            nb[:, c] = n[:, c].astype(bf16)
        for c in halves:
            m[:, c] = dot(gb[...], nb[:, c]) + gain * n[:, c] + mid * g[:, c]
            mb[:, c] = m[:, c].astype(bf16)
        return gain * mid

    def grow(level, gain):
        for c in halves:
            z[:, c] = dot(gb[...], zb[:, c]) + gain * z[:, c] + level * g[:, c]
            zb[:, c] = z[:, c].astype(bf16)
        return level * gain

    level = factor(centre)
    z[...] = g[...]
    zb[...] = gb[...]
    mu = advance(centre, level)

    def pair(_, carry):
        mu, level = carry
        gain = factor(mu)
        level = grow(level, gain)
        return advance(mu, gain), level

    mu, level = lax.fori_loop(0, 2, pair, (mu, level))
    level = grow(level, factor(mu))
    shrink = lax.rsqrt(scale)
    put(trans_ref, z[...] * shrink + jnp.where(eye(), level * shrink, 0.0))


def run_ns(core, mine, other):
    wide, narrow = pltpu.VMEM((N, N), f32), pltpu.VMEM((N, N), bf16)
    return pl.pallas_call(
        ns_kernel,
        out_shape=jax.ShapeDtypeStruct((2, N, N), bf16),
        in_specs=[SMEM, VMEM, VMEM],
        out_specs=VMEM,
        scratch_shapes=[wide, narrow, wide, narrow, narrow, wide, narrow, wide, narrow, wide, narrow],
        compiler_params=pltpu.CompilerParams(vmem_limit_bytes=20 << 20),
        cost_estimate=pl.CostEstimate(flops=40 * N**3, bytes_accessed=4 * N * N, transcendentals=0),
    )(core, mine, other)


def rotate_kernel(layer_ref, trans_ref, filt_ref, out_ref, part):
    rows = pl.ds(pl.multiple_of(layer_ref[0] * 64, 64), 64)
    part[0:64] = trans_ref[0, rows]
    part[64:128] = trans_ref[1, rows]
    for k in range(8):
        both = dot(part[...], filt_ref[k])
        rotated = (both[0:64] + both[64:128]).astype(bf16)
        for x in range(4):
            out_ref[x, k] = rotated[16 * x : 16 * x + 16]


def run_rotate(layer, trans, filt):
    return pl.pallas_call(
        rotate_kernel,
        out_shape=jax.ShapeDtypeStruct((4, 8, 16, 256), bf16),
        in_specs=[SMEM, VMEM, VMEM],
        out_specs=VMEM,
        scratch_shapes=[pltpu.VMEM((128, N), bf16)],
        compiler_params=pltpu.CompilerParams(vmem_limit_bytes=4 << 20),
    )(layer, trans, filt)


def project_kernel(core_ref, mine_ref, other_ref, trans_ref, out_ref, h, w):
    def product(a, b):
        return dot(a[0], b[0]) + dot(a[0], b[1]) + dot(a[1], b[0])

    @pl.when(core_ref[0] == 0)
    def _():
        unfold(other_ref, out_ref)

    @pl.when(core_ref[0] == 1)
    def _():
        unfold(mine_ref, out_ref)

    put(h, out_ref[...])
    put(w, product(h, trans_ref))
    out_ref[...] = product(trans_ref, w)


def run_project(core, mine, other, trans):
    return pl.pallas_call(
        project_kernel,
        out_shape=jax.ShapeDtypeStruct((N, N), f32),
        in_specs=[SMEM, VMEM, VMEM, VMEM],
        out_specs=VMEM,
        scratch_shapes=[pltpu.VMEM((2, N, N), bf16)] * 2,
        compiler_params=pltpu.CompilerParams(vmem_limit_bytes=10 << 20),
        cost_estimate=pl.CostEstimate(flops=12 * N**3, bytes_accessed=4 * N * N, transcendentals=0),
    )(core, mine, other, trans)

def exchange(array, axes):
    return lax.all_to_all(array, axes, split_axis=0, concat_axis=0, tiled=True)


def body(orbitals, potential, bounds):
    core = lax.axis_index("core").astype(jnp.int32)[None]
    swap = [(0, 1), (1, 0)]
    plane = ("x", "y")
    chip = lax.axis_index(plane).astype(jnp.int32)[None]
    layer = lax.axis_index("z").astype(jnp.int32)[None]
    bands = orbitals.reshape(8, 2, 4, 2048).transpose(0, 2, 1, 3).reshape(8, 8, 2048)
    coarse = lax.reduce_precision(potential, 8, 7)
    pieces = jnp.concatenate([coarse, potential - coarse]).astype(bf16)
    packed = jnp.concatenate([bands, jnp.broadcast_to(pieces, (8, 8, 2048))], axis=1)
    whole = exchange(packed, ("y", "core"))
    pair = run_filter(bounds, whole).reshape(256, 4, 256)
    pair = exchange(pair, ("z", "x", "y", "core"))
    near = pair.reshape(256, 2, 2, 256).transpose(1, 0, 2, 3).reshape(2, N, 256)
    column = lax.all_gather(near[0], "z")
    far = lax.ppermute(near, "core", swap)
    parts = exchange(run_gram(core, near, far).reshape(16, 8, 16, 128), plane)
    parts = exchange(run_sum(chip, parts, 8), "z")
    mine = exchange(run_sum(chip, parts, 16), plane).reshape(128, 16, 128)
    other = lax.ppermute(mine, "core", swap)
    transform = run_ns(core, mine, other)
    rotated = run_rotate(layer, transform, column)
    projected = run_project(core, mine, other, transform)
    rotated = exchange(rotated, "x")
    rotated = rotated.transpose(2, 1, 0, 3).reshape(16, 4, 2048)
    return rotated, projected


def solution(mesh):
    fine = Mesh(mesh.devices.reshape(8, 4, 4, 2), ("z", "x", "y", "core"))
    return jax.shard_map(
        body,
        mesh=fine,
        in_specs=(P(("z", "x"), ("y", "core"), None), P(("y", "core"), None), P()),
        out_specs=(P(("z", "x"), ("y", "core"), None), P()),
        check_vma=False,
    )
```

```python
import jax
import jax.numpy as jnp
from jax import lax
from jax.experimental import pallas as pl
from jax.experimental.pallas import tpu as pltpu
from jax.sharding import Mesh
from jax.sharding import PartitionSpec as P

f32, bf16 = jnp.float32, jnp.bfloat16
def shuffle_matrix():
    natural = lax.broadcasted_iota(jnp.int32, (512, 512), 0)
    spread = lax.broadcasted_iota(jnp.int32, (512, 512), 1)
    place = (natural // 32 % 4) * 128 + (natural % 32) * 4 + natural // 128
    return jnp.where(spread == place, 1.0, 0.0).astype(bf16)


def pack_kernel(orb_ref, pot_ref, out_ref, flat):
    field = pot_ref[...]
    coarse = field.astype(bf16).astype(f32)
    for d in range(8):
        rows = [orb_ref[2 * d].astype(f32), orb_ref[2 * d + 1].astype(f32), coarse, field - coarse]
        flat[16 * d : 16 * d + 16] = jnp.concatenate(rows, axis=0).astype(bf16)
    row = lax.broadcasted_iota(jnp.int32, (128, 128), 0)
    place = row % 16
    place = row - place + jnp.where(place < 8, place // 2 + 4 * (place % 2), place)
    select = jnp.where(lax.broadcasted_iota(jnp.int32, (128, 128), 1) == place, 1.0, 0.0).astype(bf16)
    for k in range(0, 2048, 512):
        mixed = jnp.dot(select, flat[:, k : k + 512], preferred_element_type=f32).astype(bf16)
        for d in range(8):
            out_ref[d, :, k : k + 512] = mixed[16 * d : 16 * d + 16]


def run_pack(orbitals, potential):
    return pl.pallas_call(
        pack_kernel,
        out_shape=jax.ShapeDtypeStruct((8, 16, 2048), bf16),
        in_specs=[pl.BlockSpec(memory_space=pltpu.VMEM)] * 2,
        out_specs=pl.BlockSpec(memory_space=pltpu.VMEM),
        scratch_shapes=[pltpu.VMEM((128, 2048), bf16)],
        compiler_params=pltpu.CompilerParams(vmem_limit_bytes=4 << 20),
    )(orbitals, potential)


def filter_kernel(bounds_ref, in_ref, mix_ref, out_ref, cur, old, pot, gain, flat):
    lower = bounds_ref[0]
    upper = bounds_ref[1]
    half = (upper - lower) / 2.0
    centre = (upper + lower) / 2.0
    inv = 1.0 / half
    sub = lax.broadcasted_iota(jnp.int32, (8, 128), 0)
    part = lax.broadcasted_iota(jnp.int32, (8, 128), 1) % 4

    def wrap(ref):
        for k in range(8):
            rows = slice(8 + 8 * k, 16 + 8 * k)
            v = ref[1, rows]
            ref[17, rows] = jnp.where(part < 3, pltpu.roll(v, 127, 1), pltpu.roll(v, 3, 1))
            v = ref[16, rows]
            ref[0, rows] = jnp.where(part > 0, pltpu.roll(v, 1, 1), pltpu.roll(v, 125, 1))

    def edges(ref, t, k, v):
        if k == 0:
            ref[t, 72:74] = v[0:2]
        if k == 7:
            ref[t, 6:8] = v[6:8]

    for b in range(4):
        for a in range(4):
            lanes = slice(128 * (4 * a + b), 128 * (4 * a + b) + 128)
            for s in range(8):
                flat[128 * b + 16 * s : 128 * b + 16 * s + 16, 128 * a : 128 * a + 128] = in_ref[s, :, lanes]

    for b in range(4):
        mixed = jnp.dot(flat[128 * b : 128 * b + 128], mix_ref[...], preferred_element_type=f32)
        for c in range(4):
            t = 4 * b + c
            for s in range(8):
                both = mixed[16 * s : 16 * s + 16, 128 * c : 128 * c + 128]
                cur[t + 1, 8 + 8 * s : 16 + 8 * s] = both[:8]
                edges(cur, t + 1, s, both[:8])
                pieces = both[8:12] + both[12:16]
                rows = jnp.broadcast_to(pieces[0:1], (8, 128))
                for x in range(1, 4):
                    rows = jnp.where(sub >= 2 * x, jnp.broadcast_to(pieces[x : x + 1], (8, 128)), rows)
                rows = rows + 3.0
                pot[t, 8 * s : 8 * s + 8] = rows
                gain[t, 8 * s : 8 * s + 8] = (rows - centre) * (2.0 * inv)
                old[t + 1, 8 + 8 * s : 16 + 8 * s] = jnp.zeros((8, 128), f32)
    wrap(cur)

    def sweep(src, emit):
        @pl.loop(0, 16, unroll=16)
        def _(t):
            for k in range(8):
                r = 8 + 8 * k
                me = src[t + 1, r : r + 8]
                total = src[t + 1, r + 2 : r + 10] + src[t + 1, r - 2 : r + 6]
                total = total + src[t + 2, r : r + 8] + src[t, r : r + 8]
                total = total + pltpu.roll(me, 124, 1) + pltpu.roll(me, 4, 1)
                emit(t, k, total, me)

    def step(src, dst, weight):
        def emit(t, k, total, me):
            r = 8 + 8 * k
            new = weight * (gain[t, 8 * k : 8 * k + 8] * me - inv * total) - dst[t + 1, r : r + 8]
            dst[t + 1, r : r + 8] = new
            edges(dst, t + 1, k, new)

        sweep(src, emit)
        wrap(dst)

    @pl.loop(0, 4)
    def _(k):
        step(cur, old, jnp.where(k == 0, 0.5, 1.0))
        step(old, cur, 1.0)

    def emit(t, k, total, me):
        old[t + 1, 8 + 8 * k : 16 + 8 * k] = pot[t, 8 * k : 8 * k + 8] * me - 0.5 * total

    sweep(cur, emit)

    for half_index, ref in enumerate((cur, old)):
        rows2 = slice(2 * half_index, 2 * half_index + 2)
        for b in range(4):
            for c in range(4):
                flat[64 * b : 64 * b + 64, 128 * c : 128 * c + 128] = ref[4 * b + c + 1, 8:72].astype(bf16)
        for b in range(4):
            plain = lax.dot_general(
                flat[64 * b : 64 * b + 64], mix_ref[...], (((1,), (1,)), ((), ())), preferred_element_type=f32
            )
            for a in range(4):
                n = 4 * a + b
                lanes = slice(128 * (n % 2), 128 * (n % 2) + 128)
                for s in range(8):
                    for x in range(4):
                        r = 8 * s + 2 * x
                        out_ref[x, n // 2, s, rows2, lanes] = plain[r : r + 2, 128 * a : 128 * a + 128].astype(bf16)


def run_filter(bounds, packed):
    return pl.pallas_call(
        filter_kernel,
        out_shape=jax.ShapeDtypeStruct((4, 8, 8, 4, 256), bf16),
        in_specs=[
            pl.BlockSpec(memory_space=pltpu.SMEM),
            pl.BlockSpec(memory_space=pltpu.VMEM),
            pl.BlockSpec(memory_space=pltpu.VMEM),
        ],
        out_specs=pl.BlockSpec(memory_space=pltpu.VMEM),
        scratch_shapes=[pltpu.VMEM((18, 80, 128), f32)] * 2
        + [pltpu.VMEM((16, 64, 128), f32)] * 2
        + [pltpu.VMEM((512, 512), bf16)],
        compiler_params=pltpu.CompilerParams(vmem_limit_bytes=10 << 20),
    )(bounds, packed, shuffle_matrix())

N = 512
VMEM = pl.BlockSpec(memory_space=pltpu.VMEM)
SMEM = pl.BlockSpec(memory_space=pltpu.SMEM)
BLOCKS = [(i, j) for i in range(4) for j in range(i + 1, 4)]


def split(x):
    hi = x.astype(bf16).astype(f32)
    return hi, x - hi


def distance(first):
    row = lax.broadcasted_iota(jnp.int32, (16, 128), 0) + first
    return (lax.broadcasted_iota(jnp.int32, (16, 128), 1) - row) & 127


def fold_pair(x):
    return jnp.concatenate(split(x), axis=0).astype(bf16)


def unfold_pair(v):
    return v[0:8] + v[8:16]


def fold_diagonal(x, apart):
    hi, lo = split(x)
    low = jnp.where(apart == 65, pltpu.roll(lo, 65, 1), pltpu.roll(lo, 64, 1))
    return jnp.where(apart <= 64, hi, low).astype(bf16)


def unfold_diagonal(v, apart):
    low = jnp.where(apart == 0, pltpu.roll(v, 63, 1), pltpu.roll(v, 64, 1))
    return v + jnp.where((apart == 0) | (apart >= 2) & (apart < 64), low, 0.0)


def gram_kernel(core_ref, near_ref, far_ref, out_ref, acc):
    dims = (((1,), (1,)), ((), ()))

    def product(right):
        for rows, cols in ((slice(0, 256), slice(0, N)), (slice(256, N), slice(256, N))):
            total = lax.dot_general(near_ref[0, rows], near_ref[right, cols], dims, preferred_element_type=f32)
            total += lax.dot_general(far_ref[0, rows], far_ref[right, cols], dims, preferred_element_type=f32)
            acc[rows, cols] = total * (1.0 / 65536.0)

    @pl.when(core_ref[0] == 0)
    def _():
        product(0)

    @pl.when(core_ref[0] == 1)
    def _():
        product(1)

    for p, (i, j) in enumerate(BLOCKS):
        for g in range(16):
            out_ref[16 * p + g] = fold_pair(acc[128 * i + 8 * g : 128 * i + 8 * g + 8, 128 * j : 128 * j + 128])
    for i in range(4):
        for g in range(8):
            rows = slice(128 * i + 16 * g, 128 * i + 16 * g + 16)
            out_ref[96 + 8 * i + g] = fold_diagonal(acc[rows, 128 * i : 128 * i + 128], distance(16 * g))


def run_gram(core, near, far):
    return pl.pallas_call(
        gram_kernel,
        out_shape=jax.ShapeDtypeStruct((128, 16, 128), bf16),
        in_specs=[SMEM, VMEM, VMEM],
        out_specs=VMEM,
        scratch_shapes=[pltpu.VMEM((N, N), f32)],
        compiler_params=pltpu.CompilerParams(vmem_limit_bytes=6 << 20),
    )(core, near, far)


def sum_kernel(chip_ref, in_ref, out_ref):
    chip = chip_ref[0]
    for u in range(8):
        total = in_ref[0, u].astype(f32)
        for k in range(1, in_ref.shape[0]):
            total = total + in_ref[k, u].astype(f32)
        apart = distance(16 * u)
        pairs = fold_pair(unfold_pair(total)).astype(f32)
        diagonal = fold_diagonal(unfold_diagonal(total, apart), apart).astype(f32)
        folded = jnp.where(chip < 12, pairs, diagonal).astype(bf16)
        for k in range(out_ref.shape[0]):
            out_ref[k, u] = folded


def run_sum(chip, parts, copies):
    return pl.pallas_call(
        sum_kernel,
        out_shape=jax.ShapeDtypeStruct((copies, 8, 16, 128), bf16),
        in_specs=[SMEM, VMEM],
        out_specs=VMEM,
        compiler_params=pltpu.CompilerParams(vmem_limit_bytes=4 << 20),
    )(chip, parts)


def unfold(ref, out):
    for p, (i, j) in enumerate(BLOCKS):
        for g in range(16):
            out[128 * i + 8 * g : 128 * i + 8 * g + 8, 128 * j : 128 * j + 128] = unfold_pair(
                ref[16 * p + g].astype(f32)
            )
        block = out[128 * i : 128 * i + 128, 128 * j : 128 * j + 128]
        out[128 * j : 128 * j + 128, 128 * i : 128 * i + 128] = block.T
    apart = lax.broadcasted_iota(jnp.int32, (128, 128), 1) - lax.broadcasted_iota(jnp.int32, (128, 128), 0)
    apart = apart & 127
    for i in range(4):
        cols = slice(128 * i, 128 * i + 128)
        for g in range(8):
            rows = slice(128 * i + 16 * g, 128 * i + 16 * g + 16)
            out[rows, cols] = unfold_diagonal(ref[96 + 8 * i + g].astype(f32), distance(16 * g))
        block = out[cols, cols]
        out[cols, cols] = jnp.where(apart <= 64, block, block.T)


def put(ref, x):
    hi, lo = split(x)
    ref[0] = hi.astype(bf16)
    ref[1] = lo.astype(bf16)


def dot(a, b):
    return jnp.dot(a, b, preferred_element_type=f32)


def eye():
    return lax.broadcasted_iota(jnp.int32, (N, N), 0) == lax.broadcasted_iota(jnp.int32, (N, N), 1)


def ns_kernel(core_ref, mine_ref, other_ref, filt_ref, rot_ref, trans_ref, m, mb, s, sb, qb, g, gb, n, nb, z, zb):
    halves = (slice(0, 256), slice(256, N))

    @pl.when(core_ref[0] == 0)
    def _():
        unfold(mine_ref, m)

    @pl.when(core_ref[0] == 1)
    def _():
        unfold(other_ref, m)

    corr = m[...]
    scale = jnp.sqrt(jnp.sum(corr * corr) + 1e-6)
    centre = jnp.sum(jnp.where(eye(), corr, 0.0)) / (N * scale)
    m[...] = m[...] / scale - jnp.where(eye(), centre, 0.0)
    mb[...] = m[...].astype(bf16)

    def factor(mu):
        square = mu * mu
        for c in halves:
            s[:, c] = dot(mb[...], mb[:, c]) + (2.0 * mu) * m[:, c]
            sb[:, c] = s[:, c].astype(bf16)
            qb[:, c] = (0.0625 * s[:, c] - 0.5625 * m[:, c]).astype(bf16)
        low = 0.0625 * square - 0.5625 * mu
        for c in halves:
            g[:, c] = (
                dot(sb[...], qb[:, c])
                + (1.6875 + low + 0.0625 * square) * s[:, c]
                - (2.4375 + 0.5625 * square) * m[:, c]
            )
            gb[:, c] = g[:, c].astype(bf16)
        return 2.25 - 2.4375 * mu + 1.6875 * square + square * low

    def advance(mu, gain):
        mid = gain * mu
        for c in halves:
            n[:, c] = dot(gb[...], mb[:, c]) + gain * m[:, c] + mu * g[:, c]
            nb[:, c] = n[:, c].astype(bf16)
        for c in halves:
            m[:, c] = dot(gb[...], nb[:, c]) + gain * n[:, c] + mid * g[:, c]
            mb[:, c] = m[:, c].astype(bf16)
        return gain * mid

    def grow(level, gain):
        for c in halves:
            z[:, c] = dot(gb[...], zb[:, c]) + gain * z[:, c] + level * g[:, c]
            zb[:, c] = z[:, c].astype(bf16)
        return level * gain

    level = factor(centre)
    z[...] = g[...]
    zb[...] = gb[...]
    mu = advance(centre, level)

    def pair(_, carry):
        mu, level = carry
        gain = factor(mu)
        level = grow(level, gain)
        return advance(mu, gain), level

    mu, level = lax.fori_loop(0, 2, pair, (mu, level))
    level = grow(level, factor(mu))
    shrink = lax.rsqrt(scale)
    put(trans_ref, z[...] * shrink + jnp.where(eye(), level * shrink, 0.0))
    rot_ref[...] = (dot(trans_ref[0], filt_ref[...]) + dot(trans_ref[1], filt_ref[...])).astype(bf16)


def run_ns(core, mine, other, filt):
    wide, narrow = pltpu.VMEM((N, N), f32), pltpu.VMEM((N, N), bf16)
    return pl.pallas_call(
        ns_kernel,
        out_shape=(jax.ShapeDtypeStruct(filt.shape, bf16), jax.ShapeDtypeStruct((2, N, N), bf16)),
        in_specs=[SMEM, VMEM, VMEM, VMEM],
        out_specs=(VMEM, VMEM),
        scratch_shapes=[wide, narrow, wide, narrow, narrow, wide, narrow, wide, narrow, wide, narrow],
        compiler_params=pltpu.CompilerParams(vmem_limit_bytes=20 << 20),
    )(core, mine, other, filt)


def project_kernel(core_ref, mine_ref, other_ref, trans_ref, out_ref, h, w):
    def product(a, b):
        return dot(a[0], b[0]) + dot(a[0], b[1]) + dot(a[1], b[0])

    @pl.when(core_ref[0] == 0)
    def _():
        unfold(other_ref, out_ref)

    @pl.when(core_ref[0] == 1)
    def _():
        unfold(mine_ref, out_ref)

    put(h, out_ref[...])
    put(w, product(h, trans_ref))
    out_ref[...] = product(trans_ref, w)


def run_project(core, mine, other, trans):
    return pl.pallas_call(
        project_kernel,
        out_shape=jax.ShapeDtypeStruct((N, N), f32),
        in_specs=[SMEM, VMEM, VMEM, VMEM],
        out_specs=VMEM,
        scratch_shapes=[pltpu.VMEM((2, N, N), bf16)] * 2,
        compiler_params=pltpu.CompilerParams(vmem_limit_bytes=10 << 20),
        cost_estimate=pl.CostEstimate(flops=12 * N**3, bytes_accessed=4 * N * N, transcendentals=0),
    )(core, mine, other, trans)

def exchange(array, axes):
    return lax.all_to_all(array, axes, split_axis=0, concat_axis=0, tiled=True)


def body(orbitals, potential, bounds):
    core = lax.axis_index("core").astype(jnp.int32)[None]
    swap = [(0, 1), (1, 0)]
    plane = ("x", "y")
    chip = lax.axis_index(plane).astype(jnp.int32)[None]
    packed, core, chip = lax.optimization_barrier((run_pack(orbitals, potential), core, chip))
    whole = exchange(packed, ("y", "core"))
    pair = run_filter(bounds, whole).reshape(256, 4, 256)
    pair = exchange(pair, ("z", "x", "y", "core"))
    near = pair.reshape(256, 2, 2, 256).transpose(1, 0, 2, 3).reshape(2, N, 256)
    far = lax.ppermute(near, "core", swap)
    parts = exchange(run_gram(core, near, far).reshape(16, 8, 16, 128), plane)
    parts = exchange(run_sum(chip, parts, 8), "z")
    mine = exchange(run_sum(chip, parts, 16), plane).reshape(128, 16, 128)
    other = lax.ppermute(mine, "core", swap)
    rotated, transform = run_ns(core, mine, other, near[0])
    projected = run_project(core, mine, other, transform)
    rotated = exchange(rotated.reshape(32, 16, 256), ("z", "x"))
    rotated = rotated.reshape(4, 8, 16, 256).transpose(2, 0, 1, 3).reshape(16, 4, 2048)
    return rotated, projected


def solution(mesh):
    fine = Mesh(mesh.devices.reshape(8, 4, 4, 2), ("z", "x", "y", "core"))
    return jax.shard_map(
        body,
        mesh=fine,
        in_specs=(P(("z", "x"), ("y", "core"), None), P(("y", "core"), None), P()),
        out_specs=(P(("z", "x"), ("y", "core"), None), P()),
        check_vma=False,
    )
```

```python
import jax
import jax.numpy as jnp
from jax import lax
from jax.experimental import pallas as pl
from jax.experimental.pallas import tpu as pltpu
from jax.sharding import Mesh
from jax.sharding import PartitionSpec as P

f32, bf16 = jnp.float32, jnp.bfloat16
def shuffle_matrix():
    natural = lax.broadcasted_iota(jnp.int32, (512, 512), 0)
    spread = lax.broadcasted_iota(jnp.int32, (512, 512), 1)
    place = (natural // 32 % 4) * 128 + (natural % 32) * 4 + natural // 128
    return jnp.where(spread == place, 1.0, 0.0).astype(bf16)


def pack_kernel(orb_hbm, pot_hbm, out_ref, orb_ref, pot_ref, flat, sems):
    bands = pltpu.make_async_copy(orb_hbm, orb_ref, sems.at[0])
    slab = pltpu.make_async_copy(pot_hbm, pot_ref, sems.at[1])
    bands.start()
    slab.start()
    slab.wait()
    bands.wait()
    field = pot_ref[...]
    coarse = field.astype(bf16).astype(f32)
    for d in range(8):
        rows = [orb_ref[2 * d].astype(f32), orb_ref[2 * d + 1].astype(f32), coarse, field - coarse]
        flat[16 * d : 16 * d + 16] = jnp.concatenate(rows, axis=0).astype(bf16)
    row = lax.broadcasted_iota(jnp.int32, (128, 128), 0)
    place = row % 16
    place = row - place + jnp.where(place < 8, place // 2 + 4 * (place % 2), place)
    select = jnp.where(lax.broadcasted_iota(jnp.int32, (128, 128), 1) == place, 1.0, 0.0).astype(bf16)
    for k in range(0, 2048, 512):
        mixed = jnp.dot(select, flat[:, k : k + 512], preferred_element_type=f32).astype(bf16)
        for d in range(8):
            out_ref[d, :, k : k + 512] = mixed[16 * d : 16 * d + 16]


def run_pack(orbitals, potential):
    return pl.pallas_call(
        pack_kernel,
        out_shape=jax.ShapeDtypeStruct((8, 16, 2048), bf16),
        in_specs=[pl.BlockSpec(memory_space=pl.ANY)] * 2,
        out_specs=pl.BlockSpec(memory_space=pltpu.VMEM),
        scratch_shapes=[
            pltpu.VMEM((16, 4, 2048), bf16),
            pltpu.VMEM((4, 2048), f32),
            pltpu.VMEM((128, 2048), bf16),
            pltpu.SemaphoreType.DMA((2,)),
        ],
        compiler_params=pltpu.CompilerParams(vmem_limit_bytes=60 << 20),
    )(orbitals, potential)


def filter_kernel(bounds_ref, in_ref, mix_ref, out_ref, cur, old, pot, gain, flat):
    lower = bounds_ref[0]
    upper = bounds_ref[1]
    half = (upper - lower) / 2.0
    centre = (upper + lower) / 2.0
    inv = 1.0 / half
    sub = lax.broadcasted_iota(jnp.int32, (8, 128), 0)
    part = lax.broadcasted_iota(jnp.int32, (8, 128), 1) % 4

    def wrap(ref):
        for k in range(8):
            rows = slice(8 + 8 * k, 16 + 8 * k)
            v = ref[1, rows]
            ref[17, rows] = jnp.where(part < 3, pltpu.roll(v, 127, 1), pltpu.roll(v, 3, 1))
            v = ref[16, rows]
            ref[0, rows] = jnp.where(part > 0, pltpu.roll(v, 1, 1), pltpu.roll(v, 125, 1))

    def edges(ref, t, k, v):
        if k == 0:
            ref[t, 72:74] = v[0:2]
        if k == 7:
            ref[t, 6:8] = v[6:8]

    for b in range(4):
        for a in range(4):
            lanes = slice(128 * (4 * a + b), 128 * (4 * a + b) + 128)
            for s in range(8):
                flat[128 * b + 16 * s : 128 * b + 16 * s + 16, 128 * a : 128 * a + 128] = in_ref[s, :, lanes]

    for b in range(4):
        mixed = jnp.dot(flat[128 * b : 128 * b + 128], mix_ref[...], preferred_element_type=f32)
        for c in range(4):
            t = 4 * b + c
            for s in range(8):
                both = mixed[16 * s : 16 * s + 16, 128 * c : 128 * c + 128]
                cur[t + 1, 8 + 8 * s : 16 + 8 * s] = both[:8]
                edges(cur, t + 1, s, both[:8])
                pieces = both[8:12] + both[12:16]
                rows = jnp.broadcast_to(pieces[0:1], (8, 128))
                for x in range(1, 4):
                    rows = jnp.where(sub >= 2 * x, jnp.broadcast_to(pieces[x : x + 1], (8, 128)), rows)
                rows = rows + 3.0
                pot[t, 8 * s : 8 * s + 8] = rows
                gain[t, 8 * s : 8 * s + 8] = (rows - centre) * (2.0 * inv)
                old[t + 1, 8 + 8 * s : 16 + 8 * s] = jnp.zeros((8, 128), f32)
    wrap(cur)

    def sweep(src, emit):
        @pl.loop(0, 16, unroll=16)
        def _(t):
            for k in range(8):
                r = 8 + 8 * k
                me = src[t + 1, r : r + 8]
                total = src[t + 1, r + 2 : r + 10] + src[t + 1, r - 2 : r + 6]
                total = total + src[t + 2, r : r + 8] + src[t, r : r + 8]
                total = total + pltpu.roll(me, 124, 1) + pltpu.roll(me, 4, 1)
                emit(t, k, total, me)

    def step(src, dst, weight):
        def emit(t, k, total, me):
            r = 8 + 8 * k
            new = weight * (gain[t, 8 * k : 8 * k + 8] * me - inv * total) - dst[t + 1, r : r + 8]
            dst[t + 1, r : r + 8] = new
            edges(dst, t + 1, k, new)

        sweep(src, emit)
        wrap(dst)

    @pl.loop(0, 4)
    def _(k):
        step(cur, old, jnp.where(k == 0, 0.5, 1.0))
        step(old, cur, 1.0)

    def emit(t, k, total, me):
        old[t + 1, 8 + 8 * k : 16 + 8 * k] = pot[t, 8 * k : 8 * k + 8] * me - 0.5 * total

    sweep(cur, emit)

    for half_index, ref in enumerate((cur, old)):
        rows2 = slice(2 * half_index, 2 * half_index + 2)
        for b in range(4):
            for c in range(4):
                flat[64 * b : 64 * b + 64, 128 * c : 128 * c + 128] = ref[4 * b + c + 1, 8:72].astype(bf16)
        for b in range(4):
            plain = lax.dot_general(
                flat[64 * b : 64 * b + 64], mix_ref[...], (((1,), (1,)), ((), ())), preferred_element_type=f32
            )
            for a in range(4):
                n = 4 * a + b
                lanes = slice(128 * (n % 2), 128 * (n % 2) + 128)
                for s in range(8):
                    for x in range(4):
                        r = 8 * s + 2 * x
                        out_ref[x, n // 2, s, rows2, lanes] = plain[r : r + 2, 128 * a : 128 * a + 128].astype(bf16)


def run_filter(bounds, packed):
    return pl.pallas_call(
        filter_kernel,
        out_shape=jax.ShapeDtypeStruct((4, 8, 8, 4, 256), bf16),
        in_specs=[
            pl.BlockSpec(memory_space=pltpu.SMEM),
            pl.BlockSpec(memory_space=pltpu.VMEM),
            pl.BlockSpec(memory_space=pltpu.VMEM),
        ],
        out_specs=pl.BlockSpec(memory_space=pltpu.VMEM),
        scratch_shapes=[pltpu.VMEM((18, 80, 128), f32)] * 2
        + [pltpu.VMEM((16, 64, 128), f32)] * 2
        + [pltpu.VMEM((512, 512), bf16)],
        compiler_params=pltpu.CompilerParams(vmem_limit_bytes=10 << 20),
    )(bounds, packed, shuffle_matrix())

N = 512
VMEM = pl.BlockSpec(memory_space=pltpu.VMEM)
SMEM = pl.BlockSpec(memory_space=pltpu.SMEM)
BLOCKS = [(i, j) for i in range(4) for j in range(i + 1, 4)]


def split(x):
    hi = x.astype(bf16).astype(f32)
    return hi, x - hi


def distance(first):
    row = lax.broadcasted_iota(jnp.int32, (16, 128), 0) + first
    return (lax.broadcasted_iota(jnp.int32, (16, 128), 1) - row) & 127


def fold_pair(x):
    return jnp.concatenate(split(x), axis=0).astype(bf16)


def unfold_pair(v):
    return v[0:8] + v[8:16]


def fold_diagonal(x, apart):
    hi, lo = split(x)
    low = jnp.where(apart == 65, pltpu.roll(lo, 65, 1), pltpu.roll(lo, 64, 1))
    return jnp.where(apart <= 64, hi, low).astype(bf16)


def unfold_diagonal(v, apart):
    low = jnp.where(apart == 0, pltpu.roll(v, 63, 1), pltpu.roll(v, 64, 1))
    return v + jnp.where((apart == 0) | (apart >= 2) & (apart < 64), low, 0.0)


def gram_kernel(core_ref, near_ref, far_ref, out_ref, acc):
    dims = (((1,), (1,)), ((), ()))

    def product(right):
        for rows, cols in ((slice(0, 256), slice(0, N)), (slice(256, N), slice(256, N))):
            total = lax.dot_general(near_ref[0, rows], near_ref[right, cols], dims, preferred_element_type=f32)
            total += lax.dot_general(far_ref[0, rows], far_ref[right, cols], dims, preferred_element_type=f32)
            acc[rows, cols] = total * (1.0 / 65536.0)

    @pl.when(core_ref[0] == 0)
    def _():
        product(0)

    @pl.when(core_ref[0] == 1)
    def _():
        product(1)

    for p, (i, j) in enumerate(BLOCKS):
        for g in range(16):
            out_ref[16 * p + g] = fold_pair(acc[128 * i + 8 * g : 128 * i + 8 * g + 8, 128 * j : 128 * j + 128])
    for i in range(4):
        for g in range(8):
            rows = slice(128 * i + 16 * g, 128 * i + 16 * g + 16)
            out_ref[96 + 8 * i + g] = fold_diagonal(acc[rows, 128 * i : 128 * i + 128], distance(16 * g))


def run_gram(core, near, far):
    return pl.pallas_call(
        gram_kernel,
        out_shape=jax.ShapeDtypeStruct((128, 16, 128), bf16),
        in_specs=[SMEM, VMEM, VMEM],
        out_specs=VMEM,
        scratch_shapes=[pltpu.VMEM((N, N), f32)],
        compiler_params=pltpu.CompilerParams(vmem_limit_bytes=6 << 20),
    )(core, near, far)


def sum_kernel(chip_ref, in_ref, out_ref):
    chip = chip_ref[0]
    for u in range(8):
        total = in_ref[0, u].astype(f32)
        for k in range(1, in_ref.shape[0]):
            total = total + in_ref[k, u].astype(f32)
        apart = distance(16 * u)
        pairs = fold_pair(unfold_pair(total)).astype(f32)
        diagonal = fold_diagonal(unfold_diagonal(total, apart), apart).astype(f32)
        folded = jnp.where(chip < 12, pairs, diagonal).astype(bf16)
        for k in range(out_ref.shape[0]):
            out_ref[k, u] = folded


def run_sum(chip, parts, copies):
    return pl.pallas_call(
        sum_kernel,
        out_shape=jax.ShapeDtypeStruct((copies, 8, 16, 128), bf16),
        in_specs=[SMEM, VMEM],
        out_specs=VMEM,
        compiler_params=pltpu.CompilerParams(vmem_limit_bytes=4 << 20),
    )(chip, parts)


def unfold(ref, out):
    for p, (i, j) in enumerate(BLOCKS):
        for g in range(16):
            out[128 * i + 8 * g : 128 * i + 8 * g + 8, 128 * j : 128 * j + 128] = unfold_pair(
                ref[16 * p + g].astype(f32)
            )
        block = out[128 * i : 128 * i + 128, 128 * j : 128 * j + 128]
        out[128 * j : 128 * j + 128, 128 * i : 128 * i + 128] = block.T
    apart = lax.broadcasted_iota(jnp.int32, (128, 128), 1) - lax.broadcasted_iota(jnp.int32, (128, 128), 0)
    apart = apart & 127
    for i in range(4):
        cols = slice(128 * i, 128 * i + 128)
        for g in range(8):
            rows = slice(128 * i + 16 * g, 128 * i + 16 * g + 16)
            out[rows, cols] = unfold_diagonal(ref[96 + 8 * i + g].astype(f32), distance(16 * g))
        block = out[cols, cols]
        out[cols, cols] = jnp.where(apart <= 64, block, block.T)


def put(ref, x):
    hi, lo = split(x)
    ref[0] = hi.astype(bf16)
    ref[1] = lo.astype(bf16)


def dot(a, b):
    return jnp.dot(a, b, preferred_element_type=f32)


def eye():
    return lax.broadcasted_iota(jnp.int32, (N, N), 0) == lax.broadcasted_iota(jnp.int32, (N, N), 1)


def ns_kernel(core_ref, mine_ref, other_ref, filt_ref, rot_ref, trans_ref, m, mb, s, sb, qb, g, gb, n, nb, z, zb):
    halves = (slice(0, 256), slice(256, N))

    @pl.when(core_ref[0] == 0)
    def _():
        unfold(mine_ref, m)

    @pl.when(core_ref[0] == 1)
    def _():
        unfold(other_ref, m)

    corr = m[...]
    scale = jnp.sqrt(jnp.sum(corr * corr) + 1e-6)
    centre = jnp.sum(jnp.where(eye(), corr, 0.0)) / (N * scale)
    m[...] = m[...] / scale - jnp.where(eye(), centre, 0.0)
    mb[...] = m[...].astype(bf16)

    def factor(mu):
        square = mu * mu
        for c in halves:
            s[:, c] = dot(mb[...], mb[:, c]) + (2.0 * mu) * m[:, c]
            sb[:, c] = s[:, c].astype(bf16)
            qb[:, c] = (0.0625 * s[:, c] - 0.5625 * m[:, c]).astype(bf16)
        low = 0.0625 * square - 0.5625 * mu
        for c in halves:
            g[:, c] = (
                dot(sb[...], qb[:, c])
                + (1.6875 + low + 0.0625 * square) * s[:, c]
                - (2.4375 + 0.5625 * square) * m[:, c]
            )
            gb[:, c] = g[:, c].astype(bf16)
        return 2.25 - 2.4375 * mu + 1.6875 * square + square * low

    def advance(mu, gain):
        mid = gain * mu
        for c in halves:
            n[:, c] = dot(gb[...], mb[:, c]) + gain * m[:, c] + mu * g[:, c]
            nb[:, c] = n[:, c].astype(bf16)
        for c in halves:
            m[:, c] = dot(gb[...], nb[:, c]) + gain * n[:, c] + mid * g[:, c]
            mb[:, c] = m[:, c].astype(bf16)
        return gain * mid

    def grow(level, gain):
        for c in halves:
            z[:, c] = dot(gb[...], zb[:, c]) + gain * z[:, c] + level * g[:, c]
            zb[:, c] = z[:, c].astype(bf16)
        return level * gain

    level = factor(centre)
    z[...] = g[...]
    zb[...] = gb[...]
    mu = advance(centre, level)

    def pair(_, carry):
        mu, level = carry
        gain = factor(mu)
        level = grow(level, gain)
        return advance(mu, gain), level

    mu, level = lax.fori_loop(0, 2, pair, (mu, level))
    level = grow(level, factor(mu))
    shrink = lax.rsqrt(scale)
    put(trans_ref, z[...] * shrink + jnp.where(eye(), level * shrink, 0.0))
    rot_ref[...] = (dot(trans_ref[0], filt_ref[...]) + dot(trans_ref[1], filt_ref[...])).astype(bf16)


def run_ns(core, mine, other, filt):
    wide, narrow = pltpu.VMEM((N, N), f32), pltpu.VMEM((N, N), bf16)
    return pl.pallas_call(
        ns_kernel,
        out_shape=(jax.ShapeDtypeStruct(filt.shape, bf16), jax.ShapeDtypeStruct((2, N, N), bf16)),
        in_specs=[SMEM, VMEM, VMEM, VMEM],
        out_specs=(VMEM, VMEM),
        scratch_shapes=[wide, narrow, wide, narrow, narrow, wide, narrow, wide, narrow, wide, narrow],
        compiler_params=pltpu.CompilerParams(vmem_limit_bytes=20 << 20),
    )(core, mine, other, filt)


def project_kernel(core_ref, mine_ref, other_ref, trans_ref, out_ref, h, w):
    def product(a, b):
        return dot(a[0], b[0]) + dot(a[0], b[1]) + dot(a[1], b[0])

    @pl.when(core_ref[0] == 0)
    def _():
        unfold(other_ref, out_ref)

    @pl.when(core_ref[0] == 1)
    def _():
        unfold(mine_ref, out_ref)

    put(h, out_ref[...])
    put(w, product(h, trans_ref))
    out_ref[...] = product(trans_ref, w)


def run_project(core, mine, other, trans):
    return pl.pallas_call(
        project_kernel,
        out_shape=jax.ShapeDtypeStruct((N, N), f32),
        in_specs=[SMEM, VMEM, VMEM, VMEM],
        out_specs=VMEM,
        scratch_shapes=[pltpu.VMEM((2, N, N), bf16)] * 2,
        compiler_params=pltpu.CompilerParams(vmem_limit_bytes=10 << 20),
        cost_estimate=pl.CostEstimate(flops=12 * N**3, bytes_accessed=4 * N * N, transcendentals=0),
    )(core, mine, other, trans)

def exchange(array, axes):
    return lax.all_to_all(array, axes, split_axis=0, concat_axis=0, tiled=True)


def body(orbitals, potential, bounds):
    core = lax.axis_index("core").astype(jnp.int32)[None]
    swap = [(0, 1), (1, 0)]
    plane = ("x", "y")
    chip = lax.axis_index(plane).astype(jnp.int32)[None]
    packed, core, chip = lax.optimization_barrier((run_pack(orbitals, potential), core, chip))
    whole = exchange(packed, ("y", "core"))
    pair = run_filter(bounds, whole).reshape(256, 4, 256)
    pair = exchange(pair, ("z", "x", "y", "core"))
    near = pair.reshape(256, 2, 2, 256).transpose(1, 0, 2, 3).reshape(2, N, 256)
    far = lax.ppermute(near, "core", swap)
    parts = exchange(run_gram(core, near, far).reshape(16, 8, 16, 128), plane)
    parts = exchange(run_sum(chip, parts, 8), "z")
    mine = exchange(run_sum(chip, parts, 16), plane).reshape(128, 16, 128)
    other = lax.ppermute(mine, "core", swap)
    rotated, transform = run_ns(core, mine, other, near[0])
    projected = run_project(core, mine, other, transform)
    rotated = exchange(rotated.reshape(32, 16, 256), ("z", "x"))
    rotated = rotated.reshape(4, 8, 16, 256).transpose(2, 0, 1, 3).reshape(16, 4, 2048)
    return rotated, projected


def solution(mesh):
    fine = Mesh(mesh.devices.reshape(8, 4, 4, 2), ("z", "x", "y", "core"))
    return jax.shard_map(
        body,
        mesh=fine,
        in_specs=(P(("z", "x"), ("y", "core"), None), P(("y", "core"), None), P()),
        out_specs=(P(("z", "x"), ("y", "core"), None), P()),
        check_vma=False,
    )
```

```python
import jax
import jax.numpy as jnp
from jax import lax
from jax.experimental import pallas as pl
from jax.experimental.pallas import tpu as pltpu
from jax.sharding import Mesh
from jax.sharding import PartitionSpec as P

f32, bf16 = jnp.float32, jnp.bfloat16
def shuffle_matrix(out):
    natural = lax.broadcasted_iota(jnp.int32, (512, 128), 0)
    spread = lax.broadcasted_iota(jnp.int32, (512, 128), 1)
    place = (natural // 32 % 4) * 128 + (natural % 32) * 4 + natural // 128
    for c in range(0, 512, 128):
        out[:, c : c + 128] = jnp.where(spread == place - c, 1.0, 0.0).astype(bf16)


def pack_kernel(orb_hbm, pot_hbm, out_ref, orb_ref, pot_ref, flat, sems):
    bands = pltpu.make_async_copy(orb_hbm, orb_ref, sems.at[0])
    slab = pltpu.make_async_copy(pot_hbm, pot_ref, sems.at[1])
    bands.start()
    slab.start()
    slab.wait()
    bands.wait()
    field = pot_ref[...]
    coarse = field.astype(bf16).astype(f32)
    for d in range(8):
        rows = [orb_ref[2 * d].astype(f32), orb_ref[2 * d + 1].astype(f32), coarse, field - coarse]
        flat[16 * d : 16 * d + 16] = jnp.concatenate(rows, axis=0).astype(bf16)
    row = lax.broadcasted_iota(jnp.int32, (128, 128), 0)
    place = row % 16
    place = row - place + jnp.where(place < 8, place // 2 + 4 * (place % 2), place)
    select = jnp.where(lax.broadcasted_iota(jnp.int32, (128, 128), 1) == place, 1.0, 0.0).astype(bf16)
    for k in range(0, 2048, 512):
        mixed = jnp.dot(select, flat[:, k : k + 512], preferred_element_type=f32).astype(bf16)
        for d in range(8):
            out_ref[d, :, k : k + 512] = mixed[16 * d : 16 * d + 16]


def run_pack(orbitals, potential):
    return pl.pallas_call(
        pack_kernel,
        out_shape=jax.ShapeDtypeStruct((8, 16, 2048), bf16),
        in_specs=[pl.BlockSpec(memory_space=pl.ANY)] * 2,
        out_specs=pl.BlockSpec(memory_space=pltpu.VMEM),
        scratch_shapes=[
            pltpu.VMEM((16, 4, 2048), bf16),
            pltpu.VMEM((4, 2048), f32),
            pltpu.VMEM((128, 2048), bf16),
            pltpu.SemaphoreType.DMA((2,)),
        ],
        compiler_params=pltpu.CompilerParams(vmem_limit_bytes=57000000),
    )(orbitals, potential)


def filter_kernel(bounds_ref, in_ref, out_ref, cur, old, pot, gain, flat, mix_ref):
    shuffle_matrix(mix_ref)
    lower = bounds_ref[0]
    upper = bounds_ref[1]
    half = (upper - lower) / 2.0
    centre = (upper + lower) / 2.0
    inv = 1.0 / half
    sub = lax.broadcasted_iota(jnp.int32, (8, 128), 0)
    part = lax.broadcasted_iota(jnp.int32, (8, 128), 1) % 4

    def wrap(ref):
        for k in range(8):
            rows = slice(8 + 8 * k, 16 + 8 * k)
            v = ref[1, rows]
            ref[17, rows] = jnp.where(part < 3, pltpu.roll(v, 127, 1), pltpu.roll(v, 3, 1))
            v = ref[16, rows]
            ref[0, rows] = jnp.where(part > 0, pltpu.roll(v, 1, 1), pltpu.roll(v, 125, 1))

    def edges(ref, t, k, v):
        if k == 0:
            ref[t, 72:74] = v[0:2]
        if k == 7:
            ref[t, 6:8] = v[6:8]

    for b in range(4):
        for a in range(4):
            lanes = slice(128 * (4 * a + b), 128 * (4 * a + b) + 128)
            for s in range(8):
                flat[128 * b + 16 * s : 128 * b + 16 * s + 16, 128 * a : 128 * a + 128] = in_ref[s, :, lanes]

    for b in range(4):
        mixed = jnp.dot(flat[128 * b : 128 * b + 128], mix_ref[...], preferred_element_type=f32)
        for c in range(4):
            t = 4 * b + c
            for s in range(8):
                both = mixed[16 * s : 16 * s + 16, 128 * c : 128 * c + 128]
                cur[t + 1, 8 + 8 * s : 16 + 8 * s] = both[:8]
                edges(cur, t + 1, s, both[:8])
                pieces = both[8:12] + both[12:16]
                rows = jnp.broadcast_to(pieces[0:1], (8, 128))
                for x in range(1, 4):
                    rows = jnp.where(sub >= 2 * x, jnp.broadcast_to(pieces[x : x + 1], (8, 128)), rows)
                rows = rows + 3.0
                pot[t, 8 * s : 8 * s + 8] = rows
                gain[t, 8 * s : 8 * s + 8] = (rows - centre) * (2.0 * inv)
                old[t + 1, 8 + 8 * s : 16 + 8 * s] = jnp.zeros((8, 128), f32)
    wrap(cur)

    def sweep(src, emit):
        @pl.loop(0, 16, unroll=16)
        def _(t):
            for k in range(8):
                r = 8 + 8 * k
                me = src[t + 1, r : r + 8]
                total = src[t + 1, r + 2 : r + 10] + src[t + 1, r - 2 : r + 6]
                total = total + src[t + 2, r : r + 8] + src[t, r : r + 8]
                total = total + pltpu.roll(me, 124, 1) + pltpu.roll(me, 4, 1)
                emit(t, k, total, me)

    def step(src, dst, weight):
        def emit(t, k, total, me):
            r = 8 + 8 * k
            new = weight * (gain[t, 8 * k : 8 * k + 8] * me - inv * total) - dst[t + 1, r : r + 8]
            dst[t + 1, r : r + 8] = new
            edges(dst, t + 1, k, new)

        sweep(src, emit)
        wrap(dst)

    @pl.loop(0, 4)
    def _(k):
        step(cur, old, jnp.where(k == 0, 0.5, 1.0))
        step(old, cur, 1.0)

    def emit(t, k, total, me):
        old[t + 1, 8 + 8 * k : 16 + 8 * k] = pot[t, 8 * k : 8 * k + 8] * me - 0.5 * total

    sweep(cur, emit)

    for half_index, ref in enumerate((cur, old)):
        rows2 = slice(2 * half_index, 2 * half_index + 2)
        for b in range(4):
            for c in range(4):
                flat[64 * b : 64 * b + 64, 128 * c : 128 * c + 128] = ref[4 * b + c + 1, 8:72].astype(bf16)
        for b in range(4):
            plain = lax.dot_general(
                flat[64 * b : 64 * b + 64], mix_ref[...], (((1,), (1,)), ((), ())), preferred_element_type=f32
            )
            for a in range(4):
                n = 4 * a + b
                lanes = slice(128 * (n % 2), 128 * (n % 2) + 128)
                for s in range(8):
                    for x in range(4):
                        r = 8 * s + 2 * x
                        out_ref[x, n // 2, s, rows2, lanes] = plain[r : r + 2, 128 * a : 128 * a + 128].astype(bf16)


def run_filter(bounds, packed):
    return pl.pallas_call(
        filter_kernel,
        out_shape=jax.ShapeDtypeStruct((4, 8, 8, 4, 256), bf16),
        in_specs=[
            pl.BlockSpec(memory_space=pltpu.SMEM),
            pl.BlockSpec(memory_space=pltpu.VMEM),
        ],
        out_specs=pl.BlockSpec(memory_space=pltpu.VMEM),
        scratch_shapes=[pltpu.VMEM((18, 80, 128), f32)] * 2
        + [pltpu.VMEM((16, 64, 128), f32)] * 2
        + [pltpu.VMEM((512, 512), bf16)] * 2,
        compiler_params=pltpu.CompilerParams(vmem_limit_bytes=10 << 20),
    )(bounds, packed)

N = 512
VMEM = pl.BlockSpec(memory_space=pltpu.VMEM)
SMEM = pl.BlockSpec(memory_space=pltpu.SMEM)
BLOCKS = [(i, j) for i in range(4) for j in range(i + 1, 4)]


def split(x):
    hi = x.astype(bf16).astype(f32)
    return hi, x - hi


def distance(first):
    row = lax.broadcasted_iota(jnp.int32, (16, 128), 0) + first
    return (lax.broadcasted_iota(jnp.int32, (16, 128), 1) - row) & 127


def fold_pair(x):
    return jnp.concatenate(split(x), axis=0).astype(bf16)


def unfold_pair(v):
    return v[0:8] + v[8:16]


def fold_diagonal(x, apart):
    hi, lo = split(x)
    low = jnp.where(apart == 65, pltpu.roll(lo, 65, 1), pltpu.roll(lo, 64, 1))
    return jnp.where(apart <= 64, hi, low).astype(bf16)


def unfold_diagonal(v, apart):
    low = jnp.where(apart == 0, pltpu.roll(v, 63, 1), pltpu.roll(v, 64, 1))
    return v + jnp.where((apart == 0) | (apart >= 2) & (apart < 64), low, 0.0)


def gram_kernel(core_ref, near_ref, far_ref, out_ref, acc):
    dims = (((1,), (1,)), ((), ()))

    def product(right):
        for rows, cols in ((slice(0, 256), slice(0, N)), (slice(256, N), slice(256, N))):
            total = lax.dot_general(near_ref[0, rows], near_ref[right, cols], dims, preferred_element_type=f32)
            total += lax.dot_general(far_ref[0, rows], far_ref[right, cols], dims, preferred_element_type=f32)
            acc[rows, cols] = total * (1.0 / 65536.0)

    @pl.when(core_ref[0] == 0)
    def _():
        product(0)

    @pl.when(core_ref[0] == 1)
    def _():
        product(1)

    for p, (i, j) in enumerate(BLOCKS):
        for g in range(16):
            out_ref[16 * p + g] = fold_pair(acc[128 * i + 8 * g : 128 * i + 8 * g + 8, 128 * j : 128 * j + 128])
    for i in range(4):
        for g in range(8):
            rows = slice(128 * i + 16 * g, 128 * i + 16 * g + 16)
            out_ref[96 + 8 * i + g] = fold_diagonal(acc[rows, 128 * i : 128 * i + 128], distance(16 * g))


def run_gram(core, near, far):
    return pl.pallas_call(
        gram_kernel,
        out_shape=jax.ShapeDtypeStruct((128, 16, 128), bf16),
        in_specs=[SMEM, VMEM, VMEM],
        out_specs=VMEM,
        scratch_shapes=[pltpu.VMEM((N, N), f32)],
        compiler_params=pltpu.CompilerParams(vmem_limit_bytes=6 << 20),
    )(core, near, far)


def sum_kernel(chip_ref, in_ref, out_ref):
    chip = chip_ref[0]
    for u in range(8):
        total = in_ref[0, u].astype(f32)
        for k in range(1, in_ref.shape[0]):
            total = total + in_ref[k, u].astype(f32)
        apart = distance(16 * u)
        pairs = fold_pair(unfold_pair(total)).astype(f32)
        diagonal = fold_diagonal(unfold_diagonal(total, apart), apart).astype(f32)
        folded = jnp.where(chip < 12, pairs, diagonal).astype(bf16)
        for k in range(out_ref.shape[0]):
            out_ref[k, u] = folded


def run_sum(chip, parts, copies):
    return pl.pallas_call(
        sum_kernel,
        out_shape=jax.ShapeDtypeStruct((copies, 8, 16, 128), bf16),
        in_specs=[SMEM, VMEM],
        out_specs=VMEM,
        compiler_params=pltpu.CompilerParams(vmem_limit_bytes=4 << 20),
    )(chip, parts)


def unfold(ref, out):
    for p, (i, j) in enumerate(BLOCKS):
        for g in range(16):
            out[128 * i + 8 * g : 128 * i + 8 * g + 8, 128 * j : 128 * j + 128] = unfold_pair(
                ref[16 * p + g].astype(f32)
            )
        block = out[128 * i : 128 * i + 128, 128 * j : 128 * j + 128]
        out[128 * j : 128 * j + 128, 128 * i : 128 * i + 128] = block.T
    apart = lax.broadcasted_iota(jnp.int32, (128, 128), 1) - lax.broadcasted_iota(jnp.int32, (128, 128), 0)
    apart = apart & 127
    for i in range(4):
        cols = slice(128 * i, 128 * i + 128)
        for g in range(8):
            rows = slice(128 * i + 16 * g, 128 * i + 16 * g + 16)
            out[rows, cols] = unfold_diagonal(ref[96 + 8 * i + g].astype(f32), distance(16 * g))
        block = out[cols, cols]
        out[cols, cols] = jnp.where(apart <= 64, block, block.T)


def put(ref, x):
    hi, lo = split(x)
    ref[0] = hi.astype(bf16)
    ref[1] = lo.astype(bf16)


def dot(a, b):
    return jnp.dot(a, b, preferred_element_type=f32)


def eye():
    return lax.broadcasted_iota(jnp.int32, (N, N), 0) == lax.broadcasted_iota(jnp.int32, (N, N), 1)


def ns_kernel(core_ref, mine_ref, other_ref, filt_ref, rot_ref, trans_ref, m, mb, s, sb, qb, g, gb, n, nb, z, zb):
    halves = (slice(0, 256), slice(256, N))

    @pl.when(core_ref[0] == 0)
    def _():
        unfold(mine_ref, m)

    @pl.when(core_ref[0] == 1)
    def _():
        unfold(other_ref, m)

    corr = m[...]
    scale = jnp.sqrt(jnp.sum(corr * corr) + 1e-6)
    centre = jnp.sum(jnp.where(eye(), corr, 0.0)) / (N * scale)
    m[...] = m[...] / scale - jnp.where(eye(), centre, 0.0)
    mb[...] = m[...].astype(bf16)

    def factor(mu):
        square = mu * mu
        for c in halves:
            s[:, c] = dot(mb[...], mb[:, c]) + (2.0 * mu) * m[:, c]
            sb[:, c] = s[:, c].astype(bf16)
            qb[:, c] = (0.0625 * s[:, c] - 0.5625 * m[:, c]).astype(bf16)
        low = 0.0625 * square - 0.5625 * mu
        for c in halves:
            g[:, c] = (
                dot(sb[...], qb[:, c])
                + (1.6875 + low + 0.0625 * square) * s[:, c]
                - (2.4375 + 0.5625 * square) * m[:, c]
            )
            gb[:, c] = g[:, c].astype(bf16)
        return 2.25 - 2.4375 * mu + 1.6875 * square + square * low

    def advance(mu, gain):
        mid = gain * mu
        for c in halves:
            n[:, c] = dot(gb[...], mb[:, c]) + gain * m[:, c] + mu * g[:, c]
            nb[:, c] = n[:, c].astype(bf16)
        for c in halves:
            m[:, c] = dot(gb[...], nb[:, c]) + gain * n[:, c] + mid * g[:, c]
            mb[:, c] = m[:, c].astype(bf16)
        return gain * mid

    def grow(level, gain):
        for c in halves:
            z[:, c] = dot(gb[...], zb[:, c]) + gain * z[:, c] + level * g[:, c]
            zb[:, c] = z[:, c].astype(bf16)
        return level * gain

    level = factor(centre)
    z[...] = g[...]
    zb[...] = gb[...]
    mu = advance(centre, level)

    def pair(_, carry):
        mu, level = carry
        gain = factor(mu)
        level = grow(level, gain)
        return advance(mu, gain), level

    mu, level = lax.fori_loop(0, 2, pair, (mu, level))
    level = grow(level, factor(mu))
    shrink = lax.rsqrt(scale)
    put(trans_ref, z[...] * shrink + jnp.where(eye(), level * shrink, 0.0))
    rot_ref[...] = (dot(trans_ref[0], filt_ref[...]) + dot(trans_ref[1], filt_ref[...])).astype(bf16)


def run_ns(core, mine, other, filt):
    wide, narrow = pltpu.VMEM((N, N), f32), pltpu.VMEM((N, N), bf16)
    return pl.pallas_call(
        ns_kernel,
        out_shape=(jax.ShapeDtypeStruct(filt.shape, bf16), jax.ShapeDtypeStruct((2, N, N), bf16)),
        in_specs=[SMEM, VMEM, VMEM, VMEM],
        out_specs=(VMEM, VMEM),
        scratch_shapes=[wide, narrow, wide, narrow, narrow, wide, narrow, wide, narrow, wide, narrow],
        compiler_params=pltpu.CompilerParams(vmem_limit_bytes=20 << 20),
    )(core, mine, other, filt)


def project_kernel(core_ref, mine_ref, other_ref, trans_ref, out_ref, h, w):
    def product(a, b):
        return dot(a[0], b[0]) + dot(a[0], b[1]) + dot(a[1], b[0])

    @pl.when(core_ref[0] == 0)
    def _():
        unfold(other_ref, out_ref)

    @pl.when(core_ref[0] == 1)
    def _():
        unfold(mine_ref, out_ref)

    put(h, out_ref[...])
    put(w, product(h, trans_ref))
    out_ref[...] = product(trans_ref, w)


def run_project(core, mine, other, trans):
    return pl.pallas_call(
        project_kernel,
        out_shape=jax.ShapeDtypeStruct((N, N), f32),
        in_specs=[SMEM, VMEM, VMEM, VMEM],
        out_specs=VMEM,
        scratch_shapes=[pltpu.VMEM((2, N, N), bf16)] * 2,
        compiler_params=pltpu.CompilerParams(vmem_limit_bytes=10 << 20),
        cost_estimate=pl.CostEstimate(flops=12 * N**3, bytes_accessed=4 * N * N, transcendentals=0),
    )(core, mine, other, trans)

def exchange(array, axes):
    return lax.all_to_all(array, axes, split_axis=0, concat_axis=0, tiled=True)


def body(orbitals, potential, bounds):
    core = lax.axis_index("core").astype(jnp.int32)[None]
    swap = [(0, 1), (1, 0)]
    plane = ("x", "y")
    chip = lax.axis_index(plane).astype(jnp.int32)[None]
    packed, core, chip = lax.optimization_barrier((run_pack(orbitals, potential), core, chip))
    whole = exchange(packed, ("y", "core"))
    pair = run_filter(bounds, whole).reshape(256, 4, 256)
    pair = exchange(pair, ("z", "x", "y", "core"))
    near = pair.reshape(256, 2, 2, 256).transpose(1, 0, 2, 3).reshape(2, N, 256)
    far = lax.ppermute(near, "core", swap)
    parts = exchange(run_gram(core, near, far).reshape(16, 8, 16, 128), plane)
    parts = exchange(run_sum(chip, parts, 8), "z")
    mine = exchange(run_sum(chip, parts, 16), plane).reshape(128, 16, 128)
    other = lax.ppermute(mine, "core", swap)
    rotated, transform = run_ns(core, mine, other, near[0])
    projected = run_project(core, mine, other, transform)
    rotated = exchange(rotated.reshape(32, 16, 256), ("z", "x"))
    rotated = rotated.reshape(4, 8, 16, 256).transpose(2, 0, 1, 3).reshape(16, 4, 2048)
    return rotated, projected


def solution(mesh):
    fine = Mesh(mesh.devices.reshape(8, 4, 4, 2), ("z", "x", "y", "core"))
    return jax.shard_map(
        body,
        mesh=fine,
        in_specs=(P(("z", "x"), ("y", "core"), None), P(("y", "core"), None), P()),
        out_specs=(P(("z", "x"), ("y", "core"), None), P()),
        check_vma=False,
    )
```
